32 devices in a mesh: ctx: 8 (over z, core), ch: 4 (over y, x).
Axes of the slice: x: 2, y: 2, z: 4, core: 2. Of those that a mesh axis runs over, the one named last changes fastest.
Arguments:
- tokens: bfloat16 [1024, 8192], P('ctx', 'ch'), may hold values from -6 to 6
- w_in: bfloat16 [8192, 3, 4096], P('ctx', None, 'ch'), may hold values from -0.0625 to 0.0625
- short_filter: float32 [3, 3, 4096], P(None, None, 'ch'), may hold values from -3 to 3
- decay_rate: float32 [256, 16], P('ch'), may hold values from 0.00048828125 to 0.1
- residue: float32 [256, 16], P('ch'), may hold values from -1.5 to 1.5
- skip: float32 [4096], P('ch'), may hold values from -6 to 6
Outputs:
- block_out: bfloat16 [1024, 4096], P('ctx', 'ch')
The draws below stay inside these ranges and needn't reach their ends.
All inputs are finite; a program needn't handle non-finite values.
Results may differ from the reference program's by a relative error of at most 0.011.
Values may be sent and summed in bfloat16 or wider, within the bound.
No kernel may reach another device: no remote copies, remote signals or barrier semaphores. Data moves between devices by JAX's collectives and lax.ppermute only.
A program may use at most 128 MiB of HBM per device.

```python
import math
import jax
import jax.numpy as jnp
from jax import lax

D = 8192
CH = 4096
GROUP = 16
ORDER = 16
SEQ = 1024
FILTERS = 256


def levels(stream_key, extent, shards, low, high):
    gain = 1.0
    for position, parts in shards:
        heights = jax.random.uniform(jax.random.fold_in(jax.random.fold_in(stream_key, 6), position), (parts,), jnp.float32, low / len(shards), high / len(shards))
        gain = gain * jnp.repeat(jnp.exp(heights), extent[position] // parts).reshape((-1,) + (1,) * (len(extent) - 1 - position))
    return gain


def gaussian(stream_key, dims, spread, bound, cuts=(), dtype=jnp.bfloat16):
    array = spread * jax.random.normal(stream_key, dims, jnp.float32)
    if cuts:
        array = array * levels(stream_key, dims, cuts, -0.22, 0.18)
    return jnp.clip(array, -bound, bound).astype(dtype)


def setup_inputs(seed: int = 0) -> dict:
    key_list = jax.random.split(jax.random.key(seed), 7)
    tokens = gaussian(key_list[0], (SEQ, D), 1.0, 6.0, ((0, 8), (1, 4)))
    w_in = gaussian(key_list[1], (D, 3, CH), D ** -0.5, 0.0625, ((0, 8), (2, 4)))
    short_filter = gaussian(key_list[2], (3, 3, CH), 0.6, 3.0, ((2, 4),), jnp.float32)
    decay_rate = jnp.clip(jnp.exp(math.log(0.1) - 5.322034 * jax.random.uniform(key_list[3], (FILTERS, ORDER), jnp.float32) ** levels(key_list[3], (FILTERS, ORDER), ((0, 4),), -0.2, 0.2)), 0.00048828125, 0.1)
    residue = gaussian(key_list[4], (FILTERS, ORDER), 0.25, 1.5, ((0, 4),), jnp.float32)
    skip = gaussian(key_list[5], (CH,), 1.0, 6.0, ((0, 4),), jnp.float32)
    return dict(tokens=tokens, w_in=w_in, short_filter=short_filter, decay_rate=decay_rate, residue=residue, skip=skip)


def reference(tokens, w_in, short_filter, decay_rate, residue, skip):
    flat_weight = w_in.reshape(D, 3 * CH).astype(jnp.float32)
    projected = jnp.dot(tokens.astype(jnp.float32), flat_weight, precision=lax.Precision.HIGHEST)
    rounded = lax.optimization_barrier(projected.astype(jnp.bfloat16))
    proj_all = rounded.astype(jnp.float32).reshape(SEQ, 3, CH)
    padded_rows = jnp.concatenate([jnp.zeros((2, 3, CH), jnp.float32), proj_all], axis=0)
    short_mixed = short_filter[0] * padded_rows[2:] + short_filter[1] * padded_rows[1:-1] + short_filter[2] * padded_rows[:-2]
    query_part = short_mixed[:, 0]
    key_part = short_mixed[:, 1]
    value_part = short_mixed[:, 2]
    gated_input = (key_part * value_part).astype(jnp.bfloat16).astype(jnp.float32)
    pole_weight = residue * jnp.sqrt(2.0 * decay_rate)
    lag_index = jnp.arange(SEQ).astype(jnp.float32)
    filter_rows = jnp.einsum('fr,frl->fl', pole_weight, jnp.exp(-decay_rate[:, :, None] * lag_index[None, None, :]), precision=lax.Precision.HIGHEST)
    per_channel = jnp.repeat(filter_rows, GROUP, axis=0).T
    fft_len = 2 * SEQ
    long_out = jnp.fft.irfft(jnp.fft.rfft(gated_input, fft_len, axis=0) * jnp.fft.rfft(per_channel, fft_len, axis=0), fft_len, axis=0)[:SEQ]
    return (query_part * (long_out + skip * gated_input)).astype(jnp.bfloat16)
```

```python
import jax
import jax.numpy as jnp
from jax import lax
from jax.experimental import pallas as pl
from jax.experimental.pallas import tpu as pltpu
from jax.sharding import PartitionSpec as P

GROUP = 16
CHUNK = 128
F32 = jnp.float32
BF16 = jnp.bfloat16


def pick(blocks, index):
    chosen = blocks[0]
    for i in range(1, len(blocks)):
        chosen = jnp.where(index == i, blocks[i], chosen)
    return chosen


def swap_cores(block, n_ctx):
    return lax.ppermute(block, "ctx", [(i, i ^ 1) for i in range(n_ctx)])


def to_plane(block, distance, planes):
    route = [(2 * z + c, 2 * (z ^ distance) + c) for z in range(planes) for c in range(2)]
    return lax.ppermute(block, "ctx", route)


def to_column(block, distance, n_ch):
    return lax.ppermute(block, "ch", [(j, j ^ distance) for j in range(n_ch)])


def spread_tokens(tokens, z, me, planes, n_ch):
    rows = tokens.shape[0] // n_ch
    pieces = tokens.reshape(n_ch, rows, tokens.shape[1])
    got = []
    for s in range(n_ch):
        piece = lax.dynamic_index_in_dim(pieces, me ^ s, 0, keepdims=False)
        got.append(to_column(piece, s, n_ch) if s else piece)
    came = []
    for u in range(planes):
        piece = pick(got, me ^ z ^ u)
        came.append(to_plane(piece, u, planes) if u else piece)
    return jnp.concatenate([pick(came, z ^ k) for k in range(planes)], axis=0)


def project_kernel(planes, where_ref, x_own, x_sib, w_own, w_sib, *outs):
    turn = pl.program_id(0)
    sums = jnp.dot(x_own[...], w_own[0], preferred_element_type=F32)
    sums += jnp.dot(x_sib[...], w_sib[0], preferred_element_type=F32)
    sums = sums.astype(BF16)
    lanes = sums.shape[1] // 2
    for r in range(planes):

        @pl.when(turn == r)
        def _():
            outs[r][0, 0] = sums[:, :lanes]
            outs[r][1, 0] = sums[:, lanes:]


def project(x, w_own, w_sib, z, core, planes):
    rows, wide = x.shape
    depth, width = w_own.shape[1:]
    across = width // planes
    lanes = across // 2
    if lanes % 128:
        halves = x.reshape(rows, 2, depth)
        x_own = lax.dynamic_index_in_dim(halves, core, 1, keepdims=False)
        x_sib = lax.dynamic_index_in_dim(halves, 1 - core, 1, keepdims=False)
        sums = jnp.einsum("tk,jkc->tjc", x_own, w_own, preferred_element_type=F32)
        sums += jnp.einsum("tk,jkc->tjc", x_sib, w_sib, preferred_element_type=F32)
        sums = sums.astype(BF16).reshape(rows, 3, planes, 2, lanes).transpose(2, 3, 1, 0, 4)
        return [
            lax.dynamic_index_in_dim(sums, (z + r) % planes, 0, keepdims=False)
            for r in range(planes)
        ]

    def out_at(r):
        def at(turn, j, where):
            return 0, jnp.where(turn == r, j, jnp.where(turn < r, 0, 2)), 0, 0

        return at

    def w_at(turn, j, where):
        return j, 0, (where[0] + turn) % planes

    return pl.pallas_call(
        lambda *refs: project_kernel(planes, *refs),
        grid_spec=pltpu.PrefetchScalarGridSpec(
            num_scalar_prefetch=1,
            grid=(planes, 3),
            in_specs=[
                pl.BlockSpec((rows, depth), lambda turn, j, where: (0, where[1])),
                pl.BlockSpec((rows, depth), lambda turn, j, where: (0, 1 - where[1])),
                pl.BlockSpec((1, depth, across), w_at),
                pl.BlockSpec((1, depth, across), w_at),
            ],
            out_specs=[pl.BlockSpec((2, 1, rows, lanes), out_at(r)) for r in range(planes)],
        ),
        out_shape=[jax.ShapeDtypeStruct((2, 3, rows, lanes), BF16)] * planes,
        compiler_params=pltpu.CompilerParams(vmem_limit_bytes=32 << 20),
        cost_estimate=pl.CostEstimate(
            flops=2 * rows * wide * 3 * width,
            bytes_accessed=2 * (wide * 3 * width + rows * wide + rows * 3 * width),
            transcendentals=0,
        ),
        name="project",
    )(jnp.stack([z, core]).astype(jnp.int32), x, x, w_own, w_sib)


def add(*blocks):
    total = blocks[0].astype(F32)
    for block in blocks[1:]:
        total = total + block.astype(F32)
    return total.astype(BF16)


def reduce_planes(streams, planes):
    last = planes - 1
    up, down = [None] * len(streams), [None] * len(streams)
    for t in range(last):
        up_route = [(2 * z + c, 2 * z + 2 + c) for z in range(min(t + 1, last)) for c in range(2)]
        down_route = [(2 * (last - z) + c, 2 * (last - z) - 2 + c) for z in range(min(t + 1, last)) for c in range(2)]
        for i, blocks in enumerate(streams):
            sent_up, sent_down = blocks[last - t], blocks[t + 1]
            if t:
                sent_up, sent_down = add(sent_up, up[i]), add(sent_down, down[i])
            up[i] = lax.ppermute(sent_up, "ctx", up_route)
            down[i] = lax.ppermute(sent_down, "ctx", down_route)
    return [add(blocks[0], up[i], down[i]) for i, blocks in enumerate(streams)]


def long_filters(decay, weight):
    lag = jnp.arange(CHUNK)
    apart = lag[:, None] - lag[None, :]
    away = jnp.maximum(apart, 0).astype(F32)
    near = jnp.sum(
        weight[:, :, None, None] * jnp.exp(-decay[:, :, None, None] * away[None, None]), axis=1
    )
    near = jnp.where(apart[None] >= 0, near, 0.0)
    poles = decay.reshape(-1)
    position = lag.astype(F32)
    collect = jnp.exp(-poles[:, None] * (CHUNK - 1 - position)[None, :])
    emit = weight.reshape(-1)[None, :] * jnp.exp(-poles[None, :] * (position + 1.0)[:, None])
    return near, collect, emit, jnp.exp(-CHUNK * poles)[:, None]


def halves_of(value):
    high = value.astype(BF16)
    return high, (value - high.astype(F32)).astype(BF16)


def mix_kernel(order, parts, planes, n_ch, where_ref, *refs):
    data, (taps, skip, near, collect, emit, keep), refs = refs[:parts], refs[parts : parts + 6], refs[parts + 6 :]
    outs, (proj, long_in, done) = refs[:planes], refs[planes:]
    core, me, z = where_ref[0], where_ref[1], where_ref[2]
    lanes = skip.shape[1]
    groups = near.shape[0]
    proj[:, 0:8] = jnp.zeros((3, 8, lanes), F32)
    rows = CHUNK // n_ch
    for (side, first, pieces), ref in zip(order, data, strict=True):
        owner = core if side == 0 else 1 - core
        for s in range(pieces):
            for k in range(planes):
                at = (2 * k + owner) * CHUNK + (me ^ (first + s)) * rows + 8
                start = (s * planes + k) * rows
                for j in range(3):
                    proj[j, pl.ds(pl.multiple_of(at, 8), rows)] = ref[j, start : start + rows].astype(F32)

    lane_group = lax.broadcasted_iota(jnp.int32, (1, lanes), 1) // GROUP
    pole_group = lax.broadcasted_iota(jnp.int32, (collect.shape[0], lanes), 0) // (collect.shape[0] // groups)
    same = pole_group == lane_group
    collect2 = jnp.concatenate(halves_of(collect[...]), axis=1)
    emit_high, emit_low = halves_of(emit[...])
    emit3 = jnp.concatenate([emit_high, emit_low, emit_high], axis=1)
    state = jnp.zeros(same.shape, F32)
    chunks = 2 * planes
    for n in range(chunks):
        mixed = []
        for j in range(3):
            total = 0.0
            for lag in range(3):
                total += taps[lag, j : j + 1] * proj[j, 8 - lag + n * CHUNK : 8 - lag + (n + 1) * CHUNK]
            mixed.append(total)
        gated = (mixed[1] * mixed[2]).astype(BF16)
        gated2 = jnp.concatenate([gated, gated], axis=0)
        long_out = skip[...] * gated.astype(F32)
        if n:
            state_high, state_low = halves_of(state)
            long_out += jnp.dot(
                emit3, jnp.concatenate([state_high, state_high, state_low], axis=0), preferred_element_type=F32
            )
        if n < chunks - 1:
            fresh = jnp.dot(collect2, gated2, preferred_element_type=F32)
            state = keep[...] * state + jnp.where(same, fresh, 0.0)
        long_in[n // 2, n % 2] = gated2
        done[n * CHUNK : (n + 1) * CHUNK] = long_out
        proj[0, 8 + n * CHUNK - 8 : n * CHUNK + CHUNK] = mixed[0]
    for g in range(groups):
        near2 = jnp.concatenate(halves_of(near[g]), axis=1)
        mine = lane_group == g
        for k in range(planes):
            pair = jnp.concatenate([long_in[k, 0], long_in[k, 1]], axis=1)
            both = jnp.dot(near2, pair, preferred_element_type=F32)
            for c in range(2):
                at = slice((2 * k + c) * CHUNK, (2 * k + c + 1) * CHUNK)
                done[at] += jnp.where(mine, both[:, c * lanes : (c + 1) * lanes], 0.0)
    for u in range(planes):
        at = pl.multiple_of((z ^ u) * 2 * CHUNK, CHUNK)
        both = proj[0, pl.ds(at, 2 * CHUNK)] * done[pl.ds(at, 2 * CHUNK)]
        outs[u][...] = both.astype(BF16).reshape(2, CHUNK, lanes)


def mix(own, sib, pieces, taps, skip, filters, core, me, z, planes, n_ch):
    lanes = skip.shape[0]
    if lanes % 128:
        return mix_plainly(own, sib, taps, skip, filters, core, me, z, planes, n_ch)
    order, data, first = [], [], 0
    for i, count in enumerate(pieces):
        order += [(0, first, count), (1, first, count)]
        data += [own[i], sib[i]]
        first += count
    poles = filters[1].shape[0]
    length = 2 * planes * CHUNK
    vmem = pl.BlockSpec(memory_space=pltpu.VMEM)
    return pl.pallas_call(
        lambda *refs: mix_kernel(order, len(data), planes, n_ch, *refs),
        in_specs=[pl.BlockSpec(memory_space=pltpu.SMEM)] + [vmem] * (len(data) + 6),
        out_specs=[vmem] * planes,
        out_shape=[jax.ShapeDtypeStruct((2, CHUNK, lanes), BF16)] * planes,
        scratch_shapes=[
            pltpu.VMEM((3, length + 8, lanes), F32),
            pltpu.VMEM((planes, 2, 2 * CHUNK, lanes), BF16),
            pltpu.VMEM((length, lanes), F32),
        ],
        compiler_params=pltpu.CompilerParams(vmem_limit_bytes=32 << 20),
        cost_estimate=pl.CostEstimate(
            flops=2 * length * lanes * (2 * CHUNK * filters[0].shape[0] + 5 * poles),
            bytes_accessed=2 * 4 * length * lanes,
            transcendentals=0,
        ),
        name="mix",
    )(
        jnp.stack([core, me, z]).astype(jnp.int32), *data, taps, skip[None], *filters
    )


def mix_plainly(own, sib, taps, skip, filters, core, me, z, planes, n_ch):
    lanes = skip.shape[0]
    near, collect, emit, keep = filters
    groups, rows = near.shape[0], CHUNK // n_ch
    sides = []
    for side in (own, sib):
        blocks = jnp.concatenate(side, axis=1).reshape(3, n_ch, planes, rows, lanes)
        sides.append(jnp.stack([lax.dynamic_index_in_dim(blocks, me ^ s, 1, keepdims=False) for s in range(n_ch)], 2))
    both = jnp.stack([pick(sides, core), pick(sides, 1 - core)], axis=2)
    proj = both.reshape(3, -1, lanes).astype(F32)
    length = proj.shape[1]
    padded = jnp.pad(proj, ((0, 0), (2, 0), (0, 0)))
    mixed = sum(taps[lag][:, None] * padded[:, 2 - lag : 2 - lag + length] for lag in range(3))
    gated = lax.optimization_barrier((mixed[1] * mixed[2]).astype(BF16)).astype(F32)
    chunks = length // CHUNK
    columns = gated.reshape(chunks, CHUNK, groups, GROUP)
    high = lax.Precision.HIGHEST
    out = jnp.einsum("gij,njgc->nigc", near, columns, precision=high)
    fresh = jnp.einsum("grj,njgc->ngrc", collect.reshape(groups, -1, CHUNK), columns, precision=high)
    state, states = jnp.zeros_like(fresh[0]), []
    for n in range(chunks):
        states.append(state)
        state = keep.reshape(groups, -1, 1) * state + fresh[n]
    out += jnp.einsum("igr,ngrc->nigc", emit.reshape(CHUNK, groups, -1), jnp.stack(states), precision=high)
    out = (mixed[0] * (out.reshape(length, lanes) + skip * gated)).astype(BF16)
    out = out.reshape(planes, 2, CHUNK, lanes)
    return [lax.dynamic_index_in_dim(out, z ^ u, 0, keepdims=False) for u in range(planes)]


def local(tokens, w_in, short_filter, decay_rate, residue, skip):
    n_ctx, n_ch = lax.axis_size("ctx"), lax.axis_size("ch")
    planes = n_ctx // 2
    ctx, me = lax.axis_index("ctx"), lax.axis_index("ch")
    z, core = ctx // 2, ctx % 2
    lanes = w_in.shape[2] // n_ctx
    groups = lanes // GROUP

    w_own = w_in.transpose(1, 0, 2)
    w_sib = swap_cores(w_own, n_ctx)
    x = [spread_tokens(tokens, z, me, planes, n_ch)]
    for s in range(1, n_ch):
        x.append(to_column(x[0], s, n_ch))
    half = n_ch // 2
    streams = [
        project(jnp.concatenate(part, axis=0), w_own, w_sib, z, core, planes) for part in (x[:half], x[half:])
    ]
    summed = reduce_planes(streams, planes)
    own = [lax.dynamic_index_in_dim(block, core, 0, keepdims=False) for block in summed]
    sib = [
        swap_cores(lax.dynamic_index_in_dim(block, 1 - core, 0, keepdims=False), n_ctx) for block in summed
    ]

    mine = lambda a, count, axis: lax.dynamic_slice_in_dim(a, ctx * count, count, axis)
    decay = mine(decay_rate, groups, 0)
    weight = mine(residue, groups, 0) * jnp.sqrt(2.0 * decay)
    outs = mix(
        own,
        sib,
        [half, n_ch - half],
        mine(short_filter, lanes, 2),
        mine(skip, lanes, 0),
        long_filters(decay, weight),
        core,
        me,
        z,
        planes,
        n_ch,
    )
    came = jnp.stack([to_plane(block, u, planes) if u else block for u, block in enumerate(outs)])
    keep = lax.dynamic_index_in_dim(came, core, 1, keepdims=False)
    given = swap_cores(lax.dynamic_index_in_dim(came, 1 - core, 1, keepdims=False), n_ctx)
    pairs = [jnp.where(core == 0, keep, given), jnp.where(core == 0, given, keep)]
    columns = [pick([pairs[c][u] for u in range(planes)], z ^ k) for k in range(planes) for c in range(2)]
    return jnp.concatenate(columns, axis=1)


def solution(mesh):
    return jax.shard_map(
        local,
        mesh=mesh,
        in_specs=(
            P("ctx", "ch"),
            P("ctx", None, "ch"),
            P(None, None, "ch"),
            P("ch", None),
            P("ch", None),
            P("ch"),
        ),
        out_specs=P("ctx", "ch"),
        check_vma=False,
    )
```

```python
import jax
import jax.numpy as jnp
from jax import lax
from jax.experimental import pallas as pl
from jax.experimental.pallas import tpu as pltpu
from jax.sharding import PartitionSpec as P

GROUP = 16
CHUNK = 128
F32 = jnp.float32
BF16 = jnp.bfloat16


def pick(blocks, index):
    chosen = blocks[0]
    for i in range(1, len(blocks)):
        chosen = jnp.where(index == i, blocks[i], chosen)
    return chosen


def swap_cores(block, n_ctx):
    return lax.ppermute(block, "ctx", [(i, i ^ 1) for i in range(n_ctx)])


def to_plane(block, distance, planes):
    route = [(2 * z + c, 2 * (z ^ distance) + c) for z in range(planes) for c in range(2)]
    return lax.ppermute(block, "ctx", route)


def to_column(block, distance, n_ch):
    return lax.ppermute(block, "ch", [(j, j ^ distance) for j in range(n_ch)])


def trade_columns(tokens, me, n_ch):
    rows = tokens.shape[0] // n_ch
    pieces = tokens.reshape(n_ch, rows, tokens.shape[1])
    got = []
    for s in range(n_ch):
        piece = lax.dynamic_index_in_dim(pieces, me ^ s, 0, keepdims=False)
        got.append(to_column(piece, s, n_ch) if s else piece)
    return got


def trade_planes(got, z, me, planes):
    came = []
    for u in range(planes):
        piece = pick(got, me ^ z ^ u)
        came.append(to_plane(piece, u, planes) if u else piece)
    return came


def sending_order(planes):
    return [planes - 1, *range(1, planes - 1), 0]


def stage_kernel(planes, where_ref, w_own, w_sib, out_ref, sems):
    z, core = where_ref[0], where_ref[1]
    depth, half = w_own.shape[1], w_own.shape[2] // 2
    lanes = half // planes
    copies = []
    for side, w in enumerate((w_own, w_sib)):
        owner = core if side == 0 else 1 - core
        rows = pl.ds(pl.multiple_of(owner * depth, depth), depth)
        for i, r in enumerate(sending_order(planes)):
            columns = pl.ds(pl.multiple_of(core * half + (z + r) % planes * lanes, lanes), lanes)
            copy = pltpu.make_async_copy(
                w.at[:, :, columns], out_ref.at[:, rows, pl.ds(i * lanes, lanes)], sems.at[side, i]
            )
            copy.start()
            copies.append(copy)
    for copy in copies:
        copy.wait()


def stage(w_own, w_sib, z, core, planes):
    depth, half = w_own.shape[1], w_own.shape[2] // 2
    lanes = half // planes
    if lanes % 128:
        w = jnp.concatenate([pick([w_own, w_sib], core), pick([w_own, w_sib], 1 - core)], axis=1)
        w = lax.dynamic_slice_in_dim(w, core * half, half, 2).reshape(3, 2 * depth, planes, lanes)
        blocks = [lax.dynamic_index_in_dim(w, (z + r) % planes, 2, keepdims=False) for r in sending_order(planes)]
        return jnp.concatenate(blocks, axis=2)
    hbm = pl.BlockSpec(memory_space=pltpu.HBM)
    return pl.pallas_call(
        lambda *refs: stage_kernel(planes, *refs),
        in_specs=[pl.BlockSpec(memory_space=pltpu.SMEM), hbm, hbm],
        out_specs=pl.BlockSpec(memory_space=pltpu.VMEM),
        out_shape=jax.ShapeDtypeStruct((3, 2 * depth, half), BF16),
        scratch_shapes=[pltpu.SemaphoreType.DMA((2, planes))],
        compiler_params=pltpu.CompilerParams(vmem_limit_bytes=8 << 20),
        cost_estimate=pl.CostEstimate(flops=0, bytes_accessed=0, transcendentals=0),
        name="stage",
    )(jnp.stack([z, core]).astype(jnp.int32), w_own, w_sib)


def project_kernel(planes, pieces, *refs):
    x_refs, w_ref, outs, x_all = refs[:pieces], refs[pieces], refs[pieces + 1 : -1], refs[-1]
    lanes = w_ref.shape[2] // planes
    at = 0
    for ref in x_refs:
        x_all[at : at + ref.shape[0]] = ref[...]
        at += ref.shape[0]
    order = sending_order(planes)
    for i in range(0, planes, 2):

        @pl.loop(0, 3)
        def _(j):
            w = w_ref[j, :, i * lanes : (i + 2) * lanes]
            sums = jnp.dot(x_all[...], w, preferred_element_type=F32).astype(BF16)
            outs[order[i]][j] = sums[:, :lanes]
            outs[order[i + 1]][j] = sums[:, lanes:]


def project(xs, w, planes):
    rows = sum(x.shape[0] for x in xs)
    wide, half = w.shape[1:]
    lanes = half // planes
    if lanes % 128:
        x = jnp.concatenate(xs, axis=0)
        sums = jnp.einsum("tk,jkc->jtc", x, w, preferred_element_type=F32).astype(BF16)
        order = sending_order(planes)
        return [sums[:, :, order.index(r) * lanes : (order.index(r) + 1) * lanes] for r in range(planes)]
    vmem = pl.BlockSpec(memory_space=pltpu.VMEM)
    return pl.pallas_call(
        lambda *refs: project_kernel(planes, len(xs), *refs),
        in_specs=[vmem] * (len(xs) + 1),
        out_specs=[vmem] * planes,
        out_shape=[jax.ShapeDtypeStruct((3, rows, lanes), BF16)] * planes,
        scratch_shapes=[pltpu.VMEM((rows, wide), BF16)],
        compiler_params=pltpu.CompilerParams(vmem_limit_bytes=8 << 20),
        cost_estimate=pl.CostEstimate(flops=0, bytes_accessed=0, transcendentals=0),
        name="project",
    )(*xs, pltpu.with_memory_space_constraint(w, pltpu.VMEM))


def add(*blocks):
    total = blocks[0].astype(F32)
    for block in blocks[1:]:
        total = total + block.astype(F32)
    return total.astype(BF16)


class LineSum:
    def __init__(self, blocks):
        self.blocks, self.last = blocks, len(blocks) - 1
        self.step, self.came = 0, None

    def send(self):
        t, last = self.step, self.last
        up, down = self.blocks[last - t], self.blocks[t + 1]
        if t:
            up, down = add(up, self.came[0]), add(down, self.came[1])
        planes = range(min(t + 1, last))
        up_route = [(2 * z + c, 2 * z + 2 + c) for z in planes for c in range(2)]
        down_route = [(2 * (last - z) + c, 2 * (last - z) - 2 + c) for z in planes for c in range(2)]
        self.came = [lax.ppermute(up, "ctx", up_route), lax.ppermute(down, "ctx", down_route)]
        self.step += 1

    def after(self, value):
        *self.came, _ = lax.optimization_barrier((*self.came, value))

    def total(self):
        return add(self.blocks[0], *self.came)


def long_filters(decay, weight):
    lag = jnp.arange(CHUNK)
    apart = lag[:, None] - lag[None, :]
    away = jnp.maximum(apart, 0).astype(F32)
    near = jnp.sum(
        weight[:, :, None, None] * jnp.exp(-decay[:, :, None, None] * away[None, None]), axis=1
    )
    near = jnp.where(apart[None] >= 0, near, 0.0)
    poles = decay.reshape(-1)
    position = lag.astype(F32)
    collect = jnp.exp(-poles[:, None] * (CHUNK - 1 - position)[None, :])
    emit = weight.reshape(-1)[None, :] * jnp.exp(-poles[None, :] * (position + 1.0)[:, None])
    return near, collect, emit


def halves_of(value):
    high = value.astype(BF16)
    return high, (value - high.astype(F32)).astype(BF16)


def mix_kernel(order, parts, planes, n_ch, where_ref, *refs):
    data, (taps, skip, near, collect, emit), refs = refs[:parts], refs[parts : parts + 5], refs[parts + 5 :]
    outs, (proj, long_in, done) = refs[:planes], refs[planes:]
    core, me, z = where_ref[0], where_ref[1], where_ref[2]
    lanes = skip.shape[1]
    groups = near.shape[0]
    proj[:, 0:8] = jnp.zeros((3, 8, lanes), F32)
    rows = CHUNK // n_ch
    for pieces, ref in zip(order, data, strict=True):
        start = 0
        for side, s, first in pieces:
            owner = core if side == 0 else 1 - core
            for k in range(first, first + planes // 2):
                at = (2 * k + owner) * CHUNK + (me ^ s) * rows + 8
                for j in range(3):
                    proj[j, pl.ds(pl.multiple_of(at, 8), rows)] = ref[j, start : start + rows].astype(F32)
                start += rows

    lane_group = lax.broadcasted_iota(jnp.int32, (1, lanes), 1) // GROUP
    pole_group = lax.broadcasted_iota(jnp.int32, (collect.shape[0], lanes), 0) // (collect.shape[0] // groups)
    same = pole_group == lane_group
    keep = collect[:, 0:1] * collect[:, CHUNK - 2 : CHUNK - 1]
    collect2 = jnp.concatenate(halves_of(collect[...]), axis=1)
    emit_high, emit_low = halves_of(emit[...])
    emit3 = jnp.concatenate([emit_high, emit_low, emit_high], axis=1)
    state = jnp.zeros(same.shape, F32)
    chunks = 2 * planes
    for n in range(chunks):
        mixed = []
        for j in range(3):
            total = 0.0
            for lag in range(3):
                total += taps[lag, j : j + 1] * proj[j, 8 - lag + n * CHUNK : 8 - lag + (n + 1) * CHUNK]
            mixed.append(total)
        gated = (mixed[1] * mixed[2]).astype(BF16)
        gated2 = jnp.concatenate([gated, gated], axis=0)
        long_out = skip[...] * gated.astype(F32)
        if n:
            state_high, state_low = halves_of(state)
            long_out += jnp.dot(
                emit3, jnp.concatenate([state_high, state_high, state_low], axis=0), preferred_element_type=F32
            )
        if n < chunks - 1:
            fresh = jnp.dot(collect2, gated2, preferred_element_type=F32)
            state = keep * state + jnp.where(same, fresh, 0.0)
        long_in[n // 2, n % 2] = gated2
        done[n * CHUNK : (n + 1) * CHUNK] = long_out
        proj[0, 8 + n * CHUNK - 8 : n * CHUNK + CHUNK] = mixed[0]
    for g in range(groups):
        near2 = jnp.concatenate(halves_of(near[g]), axis=1)
        mine = lane_group == g
        for k in range(planes):
            pair = jnp.concatenate([long_in[k, 0], long_in[k, 1]], axis=1)
            both = jnp.dot(near2, pair, preferred_element_type=F32)
            for c in range(2):
                at = slice((2 * k + c) * CHUNK, (2 * k + c + 1) * CHUNK)
                done[at] += jnp.where(mine, both[:, c * lanes : (c + 1) * lanes], 0.0)
    for u in range(planes):
        at = pl.multiple_of((z ^ u) * 2 * CHUNK, CHUNK)
        both = proj[0, pl.ds(at, 2 * CHUNK)] * done[pl.ds(at, 2 * CHUNK)]
        outs[u][...] = both.astype(BF16).reshape(2, CHUNK, lanes)


def mix(data, order, taps, skip, filters, core, me, z, planes, n_ch):
    lanes = skip.shape[1]
    if lanes % 128:
        return mix_plainly(data, order, taps, skip, filters, core, me, z, planes, n_ch)
    poles = filters[1].shape[0]
    length = 2 * planes * CHUNK
    vmem = pl.BlockSpec(memory_space=pltpu.VMEM)
    return pl.pallas_call(
        lambda *refs: mix_kernel(order, len(data), planes, n_ch, *refs),
        in_specs=[pl.BlockSpec(memory_space=pltpu.SMEM)] + [vmem] * (len(data) + 5),
        out_specs=[vmem] * planes,
        out_shape=[jax.ShapeDtypeStruct((2, CHUNK, lanes), BF16)] * planes,
        scratch_shapes=[
            pltpu.VMEM((3, length + 8, lanes), F32),
            pltpu.VMEM((planes, 2, 2 * CHUNK, lanes), BF16),
            pltpu.VMEM((length, lanes), F32),
        ],
        compiler_params=pltpu.CompilerParams(vmem_limit_bytes=8 << 20),
        cost_estimate=pl.CostEstimate(flops=0, bytes_accessed=0, transcendentals=0),
        name="mix",
    )(
        jnp.stack([core, me, z]).astype(jnp.int32), *data, taps, skip, *filters
    )


def mix_plainly(data, order, taps, skip, filters, core, me, z, planes, n_ch):
    lanes = skip.shape[1]
    near, collect, emit = filters
    keep = collect[:, 0] * collect[:, CHUNK - 2]
    groups, rows = near.shape[0], CHUNK // n_ch
    sides = [[[None, None] for _ in range(n_ch)] for _ in range(2)]
    for pieces, block in zip(order, data, strict=True):
        cut = block.reshape(3, len(pieces), planes // 2, rows, lanes)
        for i, (side, s, first) in enumerate(pieces):
            sides[side][s][first > 0] = cut[:, i]
    sides = [[jnp.concatenate(halves, axis=1) for halves in side] for side in sides]
    sides = [jnp.stack([pick(side, me ^ p) for p in range(n_ch)], axis=2) for side in sides]
    both = jnp.stack([pick(sides, core), pick(sides, 1 - core)], axis=2)
    proj = both.reshape(3, -1, lanes).astype(F32)
    length = proj.shape[1]
    padded = jnp.pad(proj, ((0, 0), (2, 0), (0, 0)))
    mixed = sum(taps[lag][:, None] * padded[:, 2 - lag : 2 - lag + length] for lag in range(3))
    gated = lax.optimization_barrier((mixed[1] * mixed[2]).astype(BF16)).astype(F32)
    chunks = length // CHUNK
    columns = gated.reshape(chunks, CHUNK, groups, GROUP)
    high = lax.Precision.HIGHEST
    out = jnp.einsum("gij,njgc->nigc", near, columns, precision=high)
    fresh = jnp.einsum("grj,njgc->ngrc", collect.reshape(groups, -1, CHUNK), columns, precision=high)
    state, states = jnp.zeros_like(fresh[0]), []
    for n in range(chunks):
        states.append(state)
        state = keep.reshape(groups, -1, 1) * state + fresh[n]
    out += jnp.einsum("igr,ngrc->nigc", emit.reshape(CHUNK, groups, -1), jnp.stack(states), precision=high)
    out = (mixed[0] * (out.reshape(length, lanes) + skip * gated)).astype(BF16)
    out = out.reshape(planes, 2, CHUNK, lanes)
    return [lax.dynamic_index_in_dim(out, z ^ u, 0, keepdims=False) for u in range(planes)]


def local(tokens, w_in, short_filter, decay_rate, residue, skip):
    n_ctx, n_ch = lax.axis_size("ctx"), lax.axis_size("ch")
    planes = n_ctx // 2
    ctx, me = lax.axis_index("ctx"), lax.axis_index("ch")
    z, core = ctx // 2, ctx % 2
    half = w_in.shape[2] // 2
    lanes = half // planes
    groups = lanes // GROUP

    block = core * planes + z
    mine = lambda a, count, axis: lax.dynamic_slice_in_dim(a, block * count, count, axis)
    decay = mine(decay_rate, groups, 0)
    filters = long_filters(decay, mine(residue, groups, 0) * jnp.sqrt(2.0 * decay))

    w_own = w_in.transpose(1, 0, 2)
    w_sib = swap_cores(w_own, n_ctx)
    got = trade_columns(tokens, me, n_ch)
    came = trade_planes(got, z, me, planes)
    w_own, w_sib, _ = lax.optimization_barrier((w_own, w_sib, got[-1]))
    w = stage(w_own, w_sib, z, core, planes)
    taps, direct = mine(short_filter, lanes, 2), mine(skip, lanes, 0)[None]
    came, filters, w, taps, direct = lax.optimization_barrier((came, filters, w, taps, direct))
    by_plane = [pick(came, z ^ k) for k in range(planes)]
    middle = planes // 2
    x = [jnp.concatenate(by_plane[:middle], axis=0), jnp.concatenate(by_plane[middle:], axis=0)]

    order = []

    def project_pieces(pieces):
        xs = [y for piece, _, _ in pieces for y in (piece, swap_cores(piece, n_ctx))]
        order.append([(side, s, h * middle) for _, s, h in pieces for side in range(2)])
        return LineSum(project(xs, w, planes))

    near = [to_column(x[0], 1, n_ch), to_column(x[1], 2, n_ch), to_column(x[1], 1, n_ch), to_column(x[0], 2, n_ch)]
    a = project_pieces([(x[0], 0, 0), (x[1], 0, 1), (near[0], 1, 0), (near[1], 2, 1)])
    far = [to_column(near[0], 2, n_ch), to_column(near[1], 1, n_ch)]
    rest = [(near[2], 1, 1), (near[3], 2, 0), (far[0], 3, 0), (far[1], 3, 1)]
    rest += [(to_column(x[h], s, n_ch), s, h) for s in range(4, n_ch) for h in range(2)]
    b = project_pieces(rest)
    streams = [a, b]
    for step in range(planes - 1):
        for stream in streams:
            stream.send()
    data = [stream.total() for stream in streams]
    outs = mix(
        data,
        order,
        taps,
        direct,
        filters,
        core,
        me,
        z,
        planes,
        n_ch,
    )
    came = [to_plane(block, u, planes) if u else block for u, block in enumerate(outs)]
    came = jnp.stack(came)
    keep = lax.dynamic_index_in_dim(came, core, 1, keepdims=False)
    given = swap_cores(lax.dynamic_index_in_dim(came, 1 - core, 1, keepdims=False), n_ctx)
    sides = [jnp.where(core == 0, keep, given), jnp.where(core == 0, given, keep)]
    columns = [pick([sides[c][u] for u in range(planes)], z ^ k) for c in range(2) for k in range(planes)]
    return jnp.concatenate(columns, axis=1)


def solution(mesh):
    return jax.shard_map(
        local,
        mesh=mesh,
        in_specs=(
            P("ctx", "ch"),
            P("ctx", None, "ch"),
            P(None, None, "ch"),
            P("ch", None),
            P("ch", None),
            P("ch"),
        ),
        out_specs=P("ctx", "ch"),
        check_vma=False,
    )
```

```python
import jax
import jax.numpy as jnp
from jax import lax
from jax.experimental import pallas as pl
from jax.experimental.pallas import tpu as pltpu
from jax.sharding import PartitionSpec as P

GROUP = 16
CHUNK = 128
F32 = jnp.float32
BF16 = jnp.bfloat16


def pick(blocks, index):
    chosen = blocks[0]
    for i in range(1, len(blocks)):
        chosen = jnp.where(index == i, blocks[i], chosen)
    return chosen


def swap_cores(block, n_ctx):
    return lax.ppermute(block, "ctx", [(i, i ^ 1) for i in range(n_ctx)])


def to_plane(block, distance, planes):
    route = [(2 * z + c, 2 * (z ^ distance) + c) for z in range(planes) for c in range(2)]
    return lax.ppermute(block, "ctx", route)


def to_column(block, distance, n_ch):
    return lax.ppermute(block, "ch", [(j, j ^ distance) for j in range(n_ch)])


def trade_columns(tokens, me, n_ch):
    rows = tokens.shape[0] // n_ch
    pieces = tokens.reshape(n_ch, rows, tokens.shape[1])
    got = []
    for s in range(n_ch):
        piece = lax.dynamic_index_in_dim(pieces, me ^ s, 0, keepdims=False)
        got.append(to_column(piece, s, n_ch) if s else piece)
    return got


def trade_planes(got, z, me, planes):
    came = []
    for u in range(planes):
        piece = pick(got, me ^ z ^ u)
        came.append(to_plane(piece, u, planes) if u else piece)
    return came


def plane_of(z, r, planes):
    return (z + (1 - 2 * (z % 2)) * r + planes) % planes


def sending_order(planes):
    return [planes - 1, *range(1, planes - 1), 0]


def stage_kernel(planes, where_ref, w_own, w_sib, out_ref, sems):
    z, core = where_ref[0], where_ref[1]
    depth, half = w_own.shape[1], w_own.shape[2] // 2
    lanes = half // planes
    copies = []
    for side, w in enumerate((w_own, w_sib)):
        owner = core if side == 0 else 1 - core
        rows = pl.ds(pl.multiple_of(owner * depth, depth), depth)
        for i, r in enumerate(sending_order(planes)):
            columns = pl.ds(pl.multiple_of(core * half + plane_of(z, r, planes) * lanes, lanes), lanes)
            copy = pltpu.make_async_copy(
                w.at[:, :, columns], out_ref.at[:, rows, pl.ds(i * lanes, lanes)], sems.at[side, i]
            )
            copy.start()
            copies.append(copy)
    for copy in copies:
        copy.wait()


def stage(w_own, w_sib, z, core, planes):
    depth, half = w_own.shape[1], w_own.shape[2] // 2
    lanes = half // planes
    if lanes % 128:
        w = jnp.concatenate([pick([w_own, w_sib], core), pick([w_own, w_sib], 1 - core)], axis=1)
        w = lax.dynamic_slice_in_dim(w, core * half, half, 2).reshape(3, 2 * depth, planes, lanes)
        blocks = [lax.dynamic_index_in_dim(w, plane_of(z, r, planes), 2, keepdims=False) for r in sending_order(planes)]
        return jnp.concatenate(blocks, axis=2)
    hbm = pl.BlockSpec(memory_space=pltpu.HBM)
    return pl.pallas_call(
        lambda *refs: stage_kernel(planes, *refs),
        in_specs=[pl.BlockSpec(memory_space=pltpu.SMEM), hbm, hbm],
        out_specs=pl.BlockSpec(memory_space=pltpu.VMEM),
        out_shape=jax.ShapeDtypeStruct((3, 2 * depth, half), BF16),
        scratch_shapes=[pltpu.SemaphoreType.DMA((2, planes))],
        compiler_params=pltpu.CompilerParams(vmem_limit_bytes=8 << 20),
        cost_estimate=pl.CostEstimate(flops=0, bytes_accessed=0, transcendentals=0),
        name="stage",
    )(jnp.stack([z, core]).astype(jnp.int32), w_own, w_sib)


def project_kernel(planes, pieces, merged, *refs):
    x_refs, w_ref, outs, x_all = refs[:pieces], refs[pieces], refs[pieces + 1 : -1], refs[-1]
    lanes = w_ref.shape[2] // planes
    if merged:
        outs = [*outs[:-1], outs[-1].at[1], outs[-1].at[0]]
    at = 0
    for ref in x_refs:
        x_all[at : at + ref.shape[0]] = ref[...]
        at += ref.shape[0]
    order = sending_order(planes)
    for i in range(0, planes, 2):

        @pl.loop(0, 3)
        def _(j):
            w = w_ref[j, :, i * lanes : (i + 2) * lanes]
            sums = jnp.dot(x_all[...], w, preferred_element_type=F32).astype(BF16)
            outs[order[i]][j] = sums[:, :lanes]
            outs[order[i + 1]][j] = sums[:, lanes:]


def project(xs, w, planes, merged):
    rows = sum(x.shape[0] for x in xs)
    wide, half = w.shape[1:]
    lanes = half // planes
    if lanes % 128:
        x = jnp.concatenate(xs, axis=0)
        sums = jnp.einsum("tk,jkc->jtc", x, w, preferred_element_type=F32).astype(BF16)
        order = sending_order(planes)
        blocks = [sums[:, :, order.index(r) * lanes : (order.index(r) + 1) * lanes] for r in range(planes)]
        return [*blocks[:-2], jnp.stack([blocks[-1], blocks[-2]])] if merged else blocks
    vmem = pl.BlockSpec(memory_space=pltpu.VMEM)
    block = jax.ShapeDtypeStruct((3, rows, lanes), BF16)
    out_shape = [block] * planes
    if merged:
        out_shape = [block] * (planes - 2) + [jax.ShapeDtypeStruct((2, 3, rows, lanes), BF16)]
    return pl.pallas_call(
        lambda *refs: project_kernel(planes, len(xs), merged, *refs),
        in_specs=[vmem] * (len(xs) + 1),
        out_specs=[vmem] * len(out_shape),
        out_shape=out_shape,
        scratch_shapes=[pltpu.VMEM((rows, wide), BF16)],
        compiler_params=pltpu.CompilerParams(vmem_limit_bytes=8 << 20),
        cost_estimate=pl.CostEstimate(flops=0, bytes_accessed=0, transcendentals=0),
        name="project",
    )(*xs, pltpu.with_memory_space_constraint(w, pltpu.VMEM))


def add(*blocks):
    total = blocks[0].astype(F32)
    for block in blocks[1:]:
        total = total + block.astype(F32)
    return total.astype(BF16)


class LineSum:
    def __init__(self, planes):
        self.planes, self.last = planes, planes - 1
        self.blocks = [[] for _ in range(planes)]
        self.even, self.odd = {-1: []}, {-1: []}

    def take(self, blocks):
        for mine, block in zip(self.blocks, blocks, strict=True):
            mine.append(block)

    def take_and_send(self, blocks):
        *blocks, first = blocks
        self.take([*blocks, first[1], first[0]])
        came = self.exchange(0, first, 0)
        for t in range(2):
            self.even.setdefault(t, []).append(came[t])
        self.odd[0] = []

    def exchange(self, t, block, first):
        route = []
        for e in range(first, self.last, 2):
            if e <= t:
                route += [(2 * e + c, 2 * e + 2 + c) for c in range(2)]
            if self.last - e - 1 <= t:
                route += [(2 * e + 2 + c, 2 * e + c) for c in range(2)]
        return lax.ppermute(block, "ctx", route) if route else None

    def send(self, t, r, came, first):
        sent = self.exchange(t, add_parts(self.blocks[r], came), first)
        return [] if sent is None else [sent]

    def send_even(self, t):
        if t not in self.even:
            self.even[t] = self.send(t, self.last - t, self.odd[t - 1], 0)

    def send_odd(self, t):
        if t not in self.odd:
            self.odd[t] = self.send(t, t + 1, self.even[t - 1], 1)

    def total(self):
        return add_parts(self.blocks[0], self.even[self.last - 1], self.odd[self.last - 1])


def add_parts(*values):
    values = [value for value in values if value]
    if len({len(value) for value in values}) > 1:
        values = [[jnp.concatenate(value, axis=1)] if len(value) > 1 else value for value in values]
    parts = [add(*blocks) if len(blocks) > 1 else blocks[0] for blocks in zip(*values, strict=True)]
    return jnp.concatenate(parts, axis=1) if len(parts) > 1 else parts[0]


def tie(first, then):
    return lax.optimization_barrier((first, then))[1]


def long_filters(decay, weight):
    lag = jnp.arange(CHUNK)
    apart = lag[:, None] - lag[None, :]
    away = jnp.maximum(apart, 0).astype(F32)
    near = jnp.sum(
        weight[:, :, None, None] * jnp.exp(-decay[:, :, None, None] * away[None, None]), axis=1
    )
    near = jnp.where(apart[None] >= 0, near, 0.0)
    poles = decay.reshape(-1)
    position = lag.astype(F32)
    collect = jnp.exp(-poles[:, None] * (CHUNK - 1 - position)[None, :])
    emit = weight.reshape(-1)[None, :] * jnp.exp(-poles[None, :] * (position + 1.0)[:, None])
    return near, collect, emit


def halves_of(value):
    high = value.astype(BF16)
    return high, (value - high.astype(F32)).astype(BF16)


def mix_kernel(order, parts, planes, n_ch, where_ref, *refs):
    data, (taps, skip, near, collect, emit), refs = refs[:parts], refs[parts : parts + 5], refs[parts + 5 :]
    outs, (proj, long_in, done) = refs[:planes], refs[planes:]
    core, me, z = where_ref[0], where_ref[1], where_ref[2]
    lanes = skip.shape[1]
    groups = near.shape[0]
    proj[:, 0:8] = jnp.zeros((3, 8, lanes), F32)
    rows = CHUNK // n_ch
    for pieces, ref in zip(order, data, strict=True):
        start = 0
        for side, s, first in pieces:
            owner = core if side == 0 else 1 - core
            for k in range(first, first + planes // 2):
                at = (2 * k + owner) * CHUNK + (me ^ s) * rows + 8
                for j in range(3):
                    proj[j, pl.ds(pl.multiple_of(at, 8), rows)] = ref[j, start : start + rows].astype(F32)
                start += rows

    lane_group = lax.broadcasted_iota(jnp.int32, (1, lanes), 1) // GROUP
    pole_group = lax.broadcasted_iota(jnp.int32, (collect.shape[0], lanes), 0) // (collect.shape[0] // groups)
    same = pole_group == lane_group
    keep = collect[:, 0:1] * collect[:, CHUNK - 2 : CHUNK - 1]
    collect2 = jnp.concatenate(halves_of(collect[...]), axis=1)
    emit_high, emit_low = halves_of(emit[...])
    emit3 = jnp.concatenate([emit_high, emit_low, emit_high], axis=1)
    state = jnp.zeros(same.shape, F32)
    chunks = 2 * planes
    for n in range(chunks):
        mixed = []
        for j in range(3):
            total = 0.0
            for lag in range(3):
                total += taps[lag, j : j + 1] * proj[j, 8 - lag + n * CHUNK : 8 - lag + (n + 1) * CHUNK]
            mixed.append(total)
        gated = (mixed[1] * mixed[2]).astype(BF16)
        gated2 = jnp.concatenate([gated, gated], axis=0)
        long_out = skip[...] * gated.astype(F32)
        if n:
            state_high, state_low = halves_of(state)
            long_out += jnp.dot(
                emit3, jnp.concatenate([state_high, state_high, state_low], axis=0), preferred_element_type=F32
            )
        if n < chunks - 1:
            fresh = jnp.dot(collect2, gated2, preferred_element_type=F32)
            state = keep * state + jnp.where(same, fresh, 0.0)
        long_in[n // 2, n % 2] = gated2
        done[n * CHUNK : (n + 1) * CHUNK] = long_out
        proj[0, 8 + n * CHUNK - 8 : n * CHUNK + CHUNK] = mixed[0]
    for g in range(groups):
        near2 = jnp.concatenate(halves_of(near[g]), axis=1)
        mine = lane_group == g
        for k in range(planes):
            pair = jnp.concatenate([long_in[k, 0], long_in[k, 1]], axis=1)
            both = jnp.dot(near2, pair, preferred_element_type=F32)
            for c in range(2):
                at = slice((2 * k + c) * CHUNK, (2 * k + c + 1) * CHUNK)
                done[at] += jnp.where(mine, both[:, c * lanes : (c + 1) * lanes], 0.0)
    for u in range(planes):
        at = pl.multiple_of((z ^ u) * 2 * CHUNK, CHUNK)
        both = proj[0, pl.ds(at, 2 * CHUNK)] * done[pl.ds(at, 2 * CHUNK)]
        outs[u][...] = both.astype(BF16).reshape(2, CHUNK, lanes)


def mix(data, order, taps, skip, filters, core, me, z, planes, n_ch):
    lanes = skip.shape[1]
    if lanes % 128:
        return mix_plainly(data, order, taps, skip, filters, core, me, z, planes, n_ch)
    poles = filters[1].shape[0]
    length = 2 * planes * CHUNK
    vmem = pl.BlockSpec(memory_space=pltpu.VMEM)
    return pl.pallas_call(
        lambda *refs: mix_kernel(order, len(data), planes, n_ch, *refs),
        in_specs=[pl.BlockSpec(memory_space=pltpu.SMEM)] + [vmem] * (len(data) + 5),
        out_specs=[vmem] * planes,
        out_shape=[jax.ShapeDtypeStruct((2, CHUNK, lanes), BF16)] * planes,
        scratch_shapes=[
            pltpu.VMEM((3, length + 8, lanes), F32),
            pltpu.VMEM((planes, 2, 2 * CHUNK, lanes), BF16),
            pltpu.VMEM((length, lanes), F32),
        ],
        compiler_params=pltpu.CompilerParams(vmem_limit_bytes=8 << 20),
        cost_estimate=pl.CostEstimate(flops=0, bytes_accessed=0, transcendentals=0),
        name="mix",
    )(
        jnp.stack([core, me, z]).astype(jnp.int32), *data, taps, skip, *filters
    )


def mix_plainly(data, order, taps, skip, filters, core, me, z, planes, n_ch):
    lanes = skip.shape[1]
    near, collect, emit = filters
    keep = collect[:, 0] * collect[:, CHUNK - 2]
    groups, rows = near.shape[0], CHUNK // n_ch
    sides = [[[None, None] for _ in range(n_ch)] for _ in range(2)]
    for pieces, block in zip(order, data, strict=True):
        cut = block.reshape(3, len(pieces), planes // 2, rows, lanes)
        for i, (side, s, first) in enumerate(pieces):
            sides[side][s][first > 0] = cut[:, i]
    sides = [[jnp.concatenate(halves, axis=1) for halves in side] for side in sides]
    sides = [jnp.stack([pick(side, me ^ p) for p in range(n_ch)], axis=2) for side in sides]
    both = jnp.stack([pick(sides, core), pick(sides, 1 - core)], axis=2)
    proj = both.reshape(3, -1, lanes).astype(F32)
    length = proj.shape[1]
    padded = jnp.pad(proj, ((0, 0), (2, 0), (0, 0)))
    mixed = sum(taps[lag][:, None] * padded[:, 2 - lag : 2 - lag + length] for lag in range(3))
    gated = lax.optimization_barrier((mixed[1] * mixed[2]).astype(BF16)).astype(F32)
    chunks = length // CHUNK
    columns = gated.reshape(chunks, CHUNK, groups, GROUP)
    high = lax.Precision.HIGHEST
    out = jnp.einsum("gij,njgc->nigc", near, columns, precision=high)
    fresh = jnp.einsum("grj,njgc->ngrc", collect.reshape(groups, -1, CHUNK), columns, precision=high)
    state, states = jnp.zeros_like(fresh[0]), []
    for n in range(chunks):
        states.append(state)
        state = keep.reshape(groups, -1, 1) * state + fresh[n]
    out += jnp.einsum("igr,ngrc->nigc", emit.reshape(CHUNK, groups, -1), jnp.stack(states), precision=high)
    out = (mixed[0] * (out.reshape(length, lanes) + skip * gated)).astype(BF16)
    out = out.reshape(planes, 2, CHUNK, lanes)
    return [lax.dynamic_index_in_dim(out, z ^ u, 0, keepdims=False) for u in range(planes)]


def local(tokens, w_in, short_filter, decay_rate, residue, skip):
    n_ctx, n_ch = lax.axis_size("ctx"), lax.axis_size("ch")
    planes = n_ctx // 2
    ctx, me = lax.axis_index("ctx"), lax.axis_index("ch")
    z, core = ctx // 2, ctx % 2
    half = w_in.shape[2] // 2
    lanes = half // planes
    groups = lanes // GROUP

    block = core * planes + z
    mine = lambda a, count, axis: lax.dynamic_slice_in_dim(a, block * count, count, axis)
    decay = mine(decay_rate, groups, 0)
    filters = long_filters(decay, mine(residue, groups, 0) * jnp.sqrt(2.0 * decay))

    w_own = w_in.transpose(1, 0, 2)
    w_sib = swap_cores(w_own, n_ctx)
    got = trade_columns(tokens, me, n_ch)
    came = trade_planes(got, z, me, planes)
    w_own, w_sib, _ = lax.optimization_barrier((w_own, w_sib, got[-1]))
    w = stage(w_own, w_sib, z, core, planes)
    taps, direct = mine(short_filter, lanes, 2), mine(skip, lanes, 0)[None]
    came, filters, w, taps, direct = lax.optimization_barrier((came, filters, w, taps, direct))
    by_plane = [pick(came, z ^ k) for k in range(planes)]
    middle = planes // 2
    x = [jnp.concatenate(by_plane[:middle], axis=0), jnp.concatenate(by_plane[middle:], axis=0)]

    order = [[], []]

    def project_pieces(stream, xs, pieces, merged):
        xs = xs + [swap_cores(y, n_ctx) for y in xs]
        order[stream].extend([(side, s, h * middle) for side in range(2) for s, h in pieces])
        return project(xs, w, planes, merged)

    near = [to_column(x[0], 1, n_ch), to_column(x[1], 2, n_ch)]
    rest = [
        to_column(jnp.concatenate([x[1], near[1]], axis=0), 1, n_ch),
        to_column(jnp.concatenate([x[0], near[0]], axis=0), 2, n_ch),
    ]
    rest += [to_column(x[h], s, n_ch) for s in range(4, n_ch) for h in range(2)]
    a, b = LineSum(planes), LineSum(planes)
    blocks = project_pieces(0, x, [(0, 0), (0, 1)], True)
    a.take_and_send(blocks)
    near = tie(blocks[0], near)
    blocks = project_pieces(0, near, [(1, 0), (2, 1)], True)
    a.take_and_send(blocks)
    rest = tie(blocks[0], rest)
    halves = [(1, 1), (3, 1), (2, 0), (3, 0)] + [(s, h) for s in range(4, n_ch) for h in range(2)]
    b.take(project_pieces(1, rest, halves, False))
    for t in range(planes - 1):
        for stream in (a, b):
            stream.send_even(t)
            stream.send_odd(t)
    data = [stream.total() for stream in (a, b)]
    outs = mix(
        data,
        order,
        taps,
        direct,
        filters,
        core,
        me,
        z,
        planes,
        n_ch,
    )
    came = [to_plane(block, u, planes) if u else block for u, block in enumerate(outs)]
    came = jnp.stack(came)
    keep = lax.dynamic_index_in_dim(came, core, 1, keepdims=False)
    given = swap_cores(lax.dynamic_index_in_dim(came, 1 - core, 1, keepdims=False), n_ctx)
    sides = [jnp.where(core == 0, keep, given), jnp.where(core == 0, given, keep)]
    columns = [pick([sides[c][u] for u in range(planes)], z ^ k) for c in range(2) for k in range(planes)]
    return jnp.concatenate(columns, axis=1)


def solution(mesh):
    return jax.shard_map(
        local,
        mesh=mesh,
        in_specs=(
            P("ctx", "ch"),
            P("ctx", None, "ch"),
            P(None, None, "ch"),
            P("ch", None),
            P("ch", None),
            P("ch"),
        ),
        out_specs=P("ctx", "ch"),
        check_vma=False,
    )
```

```python
import jax
import jax.numpy as jnp
from jax import lax
from jax.experimental import pallas as pl
from jax.experimental.pallas import tpu as pltpu
from jax.sharding import PartitionSpec as P

GROUP = 16
CHUNK = 128
F32 = jnp.float32
BF16 = jnp.bfloat16


def pick(blocks, index):
    chosen = blocks[0]
    for i in range(1, len(blocks)):
        chosen = jnp.where(index == i, blocks[i], chosen)
    return chosen


def swap_cores(block, n_ctx):
    return lax.ppermute(block, "ctx", [(i, i ^ 1) for i in range(n_ctx)])


def to_plane(block, distance, planes):
    route = [(2 * z + c, 2 * (z ^ distance) + c) for z in range(planes) for c in range(2)]
    return lax.ppermute(block, "ctx", route)


def to_column(block, distance, n_ch):
    return lax.ppermute(block, "ch", [(j, j ^ distance) for j in range(n_ch)])


def trade_columns(tokens, me, n_ch):
    rows = tokens.shape[0] // n_ch
    pieces = tokens.reshape(n_ch, rows, tokens.shape[1])
    got = []
    for s in range(n_ch):
        piece = lax.dynamic_index_in_dim(pieces, me ^ s, 0, keepdims=False)
        got.append(to_column(piece, s, n_ch) if s else piece)
    return got


def trade_planes(got, z, me, planes):
    came = []
    for u in range(planes):
        piece = pick(got, me ^ z ^ u)
        came.append(to_plane(piece, u, planes) if u else piece)
    return came


def plane_of(z, r, planes):
    return (z + (1 - 2 * (z % 2)) * r + planes) % planes


def sending_order(planes):
    return [planes - 1, *range(1, planes - 1), 0]


def stage_kernel(planes, where_ref, w_own, w_sib, out_ref, sems):
    z, core = where_ref[0], where_ref[1]
    depth, half = w_own.shape[1], w_own.shape[2] // 2
    lanes = half // planes
    copies = []
    for side, w in enumerate((w_own, w_sib)):
        owner = core if side == 0 else 1 - core
        rows = pl.ds(pl.multiple_of(owner * depth, depth), depth)
        for i, r in enumerate(sending_order(planes)):
            columns = pl.ds(pl.multiple_of(core * half + plane_of(z, r, planes) * lanes, lanes), lanes)
            copy = pltpu.make_async_copy(
                w.at[:, :, columns], out_ref.at[:, rows, pl.ds(i * lanes, lanes)], sems.at[side, i]
            )
            copy.start()
            copies.append(copy)
    for copy in copies:
        copy.wait()


def stage(w_own, w_sib, z, core, planes):
    depth, half = w_own.shape[1], w_own.shape[2] // 2
    lanes = half // planes
    if lanes % 128:
        w = jnp.concatenate([pick([w_own, w_sib], core), pick([w_own, w_sib], 1 - core)], axis=1)
        w = lax.dynamic_slice_in_dim(w, core * half, half, 2).reshape(3, 2 * depth, planes, lanes)
        blocks = [lax.dynamic_index_in_dim(w, plane_of(z, r, planes), 2, keepdims=False) for r in sending_order(planes)]
        return jnp.concatenate(blocks, axis=2)
    hbm = pl.BlockSpec(memory_space=pltpu.HBM)
    return pl.pallas_call(
        lambda *refs: stage_kernel(planes, *refs),
        in_specs=[pl.BlockSpec(memory_space=pltpu.SMEM), hbm, hbm],
        out_specs=pl.BlockSpec(memory_space=pltpu.VMEM),
        out_shape=jax.ShapeDtypeStruct((3, 2 * depth, half), BF16),
        scratch_shapes=[pltpu.SemaphoreType.DMA((2, planes))],
        compiler_params=pltpu.CompilerParams(vmem_limit_bytes=8 << 20),
        cost_estimate=pl.CostEstimate(flops=0, bytes_accessed=0, transcendentals=0),
        name="stage",
    )(jnp.stack([z, core]).astype(jnp.int32), w_own, w_sib)


def project_kernel(planes, pieces, merged, *refs):
    x_refs, w_ref, outs, x_all = refs[:pieces], refs[pieces], refs[pieces + 1 : -1], refs[-1]
    lanes = w_ref.shape[2] // planes
    if merged:
        outs = [*outs[:-1], outs[-1].at[1], outs[-1].at[0]]
    at = 0
    for ref in x_refs:
        x_all[at : at + ref.shape[0]] = ref[...]
        at += ref.shape[0]
    order = sending_order(planes)
    for i in range(0, planes, 2):

        @pl.loop(0, 3)
        def _(j):
            w = w_ref[j, :, i * lanes : (i + 2) * lanes]
            sums = jnp.dot(x_all[...], w, preferred_element_type=F32).astype(BF16)
            outs[order[i]][j] = sums[:, :lanes]
            outs[order[i + 1]][j] = sums[:, lanes:]


def project(xs, w, planes, merged):
    rows = sum(x.shape[0] for x in xs)
    wide, half = w.shape[1:]
    lanes = half // planes
    if lanes % 128:
        x = jnp.concatenate(xs, axis=0)
        sums = jnp.einsum("tk,jkc->jtc", x, w, preferred_element_type=F32).astype(BF16)
        order = sending_order(planes)
        blocks = [sums[:, :, order.index(r) * lanes : (order.index(r) + 1) * lanes] for r in range(planes)]
        return [*blocks[:-2], jnp.stack([blocks[-1], blocks[-2]])] if merged else blocks
    vmem = pl.BlockSpec(memory_space=pltpu.VMEM)
    block = jax.ShapeDtypeStruct((3, rows, lanes), BF16)
    out_shape = [block] * planes
    if merged:
        out_shape = [block] * (planes - 2) + [jax.ShapeDtypeStruct((2, 3, rows, lanes), BF16)]
    return pl.pallas_call(
        lambda *refs: project_kernel(planes, len(xs), merged, *refs),
        in_specs=[vmem] * (len(xs) + 1),
        out_specs=[vmem] * len(out_shape),
        out_shape=out_shape,
        scratch_shapes=[pltpu.VMEM((rows, wide), BF16)],
        compiler_params=pltpu.CompilerParams(vmem_limit_bytes=8 << 20),
        cost_estimate=pl.CostEstimate(flops=0, bytes_accessed=0, transcendentals=0),
        name="project",
    )(*xs, pltpu.with_memory_space_constraint(w, pltpu.VMEM))


def add(*blocks):
    total = blocks[0].astype(F32)
    for block in blocks[1:]:
        total = total + block.astype(F32)
    return total.astype(BF16)


class LineSum:
    def __init__(self, planes):
        self.planes, self.last = planes, planes - 1
        self.blocks = [[] for _ in range(planes)]
        self.even, self.odd = {-1: []}, {-1: []}

    def take(self, blocks):
        for mine, block in zip(self.blocks, blocks, strict=True):
            mine.append(block)

    def take_and_send(self, blocks):
        *blocks, first = blocks
        self.take([*blocks, first[1], first[0]])
        came = self.exchange(0, first, 0)
        for t in range(2):
            self.even.setdefault(t, []).append(came[t])
        self.odd[0] = []

    def exchange(self, t, block, first):
        route = []
        for e in range(first, self.last, 2):
            if e <= t:
                route += [(2 * e + c, 2 * e + 2 + c) for c in range(2)]
            if self.last - e - 1 <= t:
                route += [(2 * e + 2 + c, 2 * e + c) for c in range(2)]
        return lax.ppermute(block, "ctx", route) if route else None

    def send(self, t, r, came, first):
        sent = self.exchange(t, add_parts(self.blocks[r], came), first)
        return [] if sent is None else [sent]

    def send_even(self, t):
        if t not in self.even:
            self.even[t] = self.send(t, self.last - t, self.odd[t - 1], 0)

    def send_odd(self, t):
        if t not in self.odd:
            self.odd[t] = self.send(t, t + 1, self.even[t - 1], 1)


def finish(streams, cuts):
    last = streams[0].last
    t = last - 1
    for stream in streams:
        stream.send_even(t)
    odd = [add_parts(stream.blocks[t + 1], stream.even[t - 1]) for stream in streams]
    whole = lambda value: jnp.concatenate(value, axis=1) if len(value) > 1 else value[0]
    near = [(whole(stream.blocks[0]), whole(stream.even[t])) for stream in streams]
    terms = []
    for cut in cuts:
        came = streams[0].exchange(t, jnp.concatenate([block[cut] for block in odd], axis=1), 1)
        row, of_cut = 0, []
        for block, even in near:
            of_cut.append([(block, cut.start, 0), (even, cut.start, 0), (came, 0, row)])
            row += block.shape[1]
        terms.append(of_cut)
    return terms


def add_parts(*values):
    values = [value for value in values if value]
    if len({len(value) for value in values}) > 1:
        values = [[jnp.concatenate(value, axis=1)] if len(value) > 1 else value for value in values]
    parts = [add(*blocks) if len(blocks) > 1 else blocks[0] for blocks in zip(*values, strict=True)]
    return jnp.concatenate(parts, axis=1) if len(parts) > 1 else parts[0]


def tie(first, then):
    return lax.optimization_barrier((first, then))[1]


def long_filters(decay, weight):
    lag = jnp.arange(CHUNK)
    apart = lag[:, None] - lag[None, :]
    away = jnp.maximum(apart, 0).astype(F32)
    near = jnp.sum(
        weight[:, :, None, None] * jnp.exp(-decay[:, :, None, None] * away[None, None]), axis=1
    )
    near = jnp.where(apart[None] >= 0, near, 0.0)
    poles = decay.reshape(-1)
    position = lag.astype(F32)
    collect = jnp.exp(-poles[:, None] * (CHUNK - 1 - position)[None, :])
    emit = weight.reshape(-1)[None, :] * jnp.exp(-poles[None, :] * (position + 1.0)[:, None])
    return near, collect, emit


def halves_of(value):
    high = value.astype(BF16)
    return high, (value - high.astype(F32)).astype(BF16)


def unpack(data):
    arrays, places = [], []
    for terms in data:
        places.append([])
        for array, plane, row in terms:
            at = next((i for i, known in enumerate(arrays) if known is array), len(arrays))
            arrays += [array] if at == len(arrays) else []
            places[-1].append((at, plane, row))
    return arrays, places


def place(order, data, refs, count, proj, where_ref, planes, n_ch):
    core, me = where_ref[0], where_ref[1]
    proj[:, 0:8] = jnp.zeros((count, 8, proj.shape[2]), F32)
    rows = CHUNK // n_ch
    for pieces, terms in zip(order, data, strict=True):
        start = 0
        for side, s, k0 in pieces:
            owner = core if side == 0 else 1 - core
            for k in range(k0, k0 + planes // 2):
                at = pl.multiple_of((2 * k + owner) * CHUNK + (me ^ s) * rows + 8, 8)
                for j in range(count):
                    total = add(*(refs[i][plane + j, row + start : row + start + rows] for i, plane, row in terms))
                    proj[j, pl.ds(at, rows)] = total.astype(F32)
                start += rows


def short_mix(taps, j, proj, at, n):
    total = 0.0
    for lag in range(3):
        total += taps[lag, j : j + 1] * proj[at, 8 - lag + n * CHUNK : 8 - lag + (n + 1) * CHUNK]
    return total


def convolve_kernel(order, data, count, planes, n_ch, where_ref, *refs):
    taps, skip, near, collect, emit, done, proj, long_in = refs[count:]
    lanes = skip.shape[1]
    groups = near.shape[0]
    place(order, data, refs, 2, proj, where_ref, planes, n_ch)

    lane_group = lax.broadcasted_iota(jnp.int32, (1, lanes), 1) // GROUP
    pole_group = lax.broadcasted_iota(jnp.int32, (collect.shape[0], lanes), 0) // (collect.shape[0] // groups)
    same = pole_group == lane_group
    keep = collect[:, 0:1] * collect[:, CHUNK - 2 : CHUNK - 1]
    collect2 = jnp.concatenate(halves_of(collect[...]), axis=1)
    emit_high, emit_low = halves_of(emit[...])
    emit3 = jnp.concatenate([emit_high, emit_low, emit_high], axis=1)
    state = jnp.zeros(same.shape, F32)
    chunks = 2 * planes
    for n in range(chunks):
        gated = (short_mix(taps, 1, proj, 0, n) * short_mix(taps, 2, proj, 1, n)).astype(BF16)
        gated2 = jnp.concatenate([gated, gated], axis=0)
        long_out = skip[...] * gated.astype(F32)
        if n:
            state_high, state_low = halves_of(state)
            long_out += jnp.dot(
                emit3, jnp.concatenate([state_high, state_high, state_low], axis=0), preferred_element_type=F32
            )
        if n < chunks - 1:
            fresh = jnp.dot(collect2, gated2, preferred_element_type=F32)
            state = keep * state + jnp.where(same, fresh, 0.0)
        long_in[n // 2, n % 2] = gated2
        done[n * CHUNK : (n + 1) * CHUNK] = long_out
    for g in range(groups):
        near2 = jnp.concatenate(halves_of(near[g]), axis=1)
        mine = lane_group == g
        for k in range(planes):
            pair = jnp.concatenate([long_in[k, 0], long_in[k, 1]], axis=1)
            both = jnp.dot(near2, pair, preferred_element_type=F32)
            for c in range(2):
                at = slice((2 * k + c) * CHUNK, (2 * k + c + 1) * CHUNK)
                done[at] += jnp.where(mine, both[:, c * lanes : (c + 1) * lanes], 0.0)


def convolve(data, order, taps, skip, filters, where, planes, n_ch):
    lanes = skip.shape[1]
    length = 2 * planes * CHUNK
    if lanes % 128:
        mixed = mix_plainly(data, order, 2, taps[:, 1:], where, planes, n_ch)
        return convolve_plainly(mixed, skip, filters)
    vmem = pl.BlockSpec(memory_space=pltpu.VMEM)
    arrays, data = unpack(data)
    return pl.pallas_call(
        lambda *refs: convolve_kernel(order, data, len(arrays), planes, n_ch, *refs),
        in_specs=[pl.BlockSpec(memory_space=pltpu.SMEM)] + [vmem] * (len(arrays) + 5),
        out_specs=vmem,
        out_shape=jax.ShapeDtypeStruct((length, lanes), F32),
        scratch_shapes=[
            pltpu.VMEM((2, length + 8, lanes), F32),
            pltpu.VMEM((planes, 2, 2 * CHUNK, lanes), BF16),
        ],
        compiler_params=pltpu.CompilerParams(vmem_limit_bytes=8 << 20),
        cost_estimate=pl.CostEstimate(flops=0, bytes_accessed=0, transcendentals=0),
        name="convolve",
    )(where, *arrays, taps, skip, *filters)


def gate_kernel(order, data, count, planes, n_ch, where_ref, *refs):
    taps, long_out = refs[count : count + 2]
    outs, (proj, done) = refs[count + 2 : -2], refs[-2:]
    z = where_ref[2]
    place(order, data, refs, 1, proj, where_ref, planes, n_ch)
    for n in range(2 * planes):
        at = slice(n * CHUNK, (n + 1) * CHUNK)
        done[at] = (short_mix(taps, 0, proj, 0, n) * long_out[at]).astype(BF16)
    for u in range(planes):
        at = pl.multiple_of((z ^ u) * 2 * CHUNK, CHUNK)
        outs[u][...] = done[pl.ds(at, 2 * CHUNK)].reshape(outs[u].shape)


def gate(data, order, taps, long_out, where, planes, n_ch):
    length, lanes = long_out.shape
    if lanes % 128:
        mixed = mix_plainly(data, order, 1, taps[:, :1], where, planes, n_ch)
        out = (mixed[0] * long_out).astype(BF16).reshape(planes, 2, CHUNK, lanes)
        return [lax.dynamic_index_in_dim(out, where[2] ^ u, 0, keepdims=False) for u in range(planes)]
    vmem = pl.BlockSpec(memory_space=pltpu.VMEM)
    arrays, data = unpack(data)
    return pl.pallas_call(
        lambda *refs: gate_kernel(order, data, len(arrays), planes, n_ch, *refs),
        in_specs=[pl.BlockSpec(memory_space=pltpu.SMEM)] + [vmem] * (len(arrays) + 2),
        out_specs=[vmem] * planes,
        out_shape=[jax.ShapeDtypeStruct((2, CHUNK, lanes), BF16)] * planes,
        scratch_shapes=[pltpu.VMEM((1, length + 8, lanes), F32), pltpu.VMEM((length, lanes), BF16)],
        compiler_params=pltpu.CompilerParams(vmem_limit_bytes=8 << 20),
        cost_estimate=pl.CostEstimate(flops=0, bytes_accessed=0, transcendentals=0),
        name="gate",
    )(where, *arrays, taps, long_out)


def mix_plainly(data, order, count, taps, where, planes, n_ch):
    core, me = where[0], where[1]
    lanes = taps.shape[2]
    length = [terms[0][0].shape[1] for terms in data]
    data = [
        add(*(array[plane : plane + count, row : row + rows] for array, plane, row in terms))
        for terms, rows in zip(data, length, strict=True)
    ]
    rows = CHUNK // n_ch
    sides = [[[None, None] for _ in range(n_ch)] for _ in range(2)]
    for pieces, block in zip(order, data, strict=True):
        cut = block.reshape(count, len(pieces), planes // 2, rows, lanes)
        for i, (side, s, first) in enumerate(pieces):
            sides[side][s][first > 0] = cut[:, i]
    sides = [[jnp.concatenate(halves, axis=1) for halves in side] for side in sides]
    sides = [jnp.stack([pick(side, me ^ p) for p in range(n_ch)], axis=2) for side in sides]
    both = jnp.stack([pick(sides, core), pick(sides, 1 - core)], axis=2)
    proj = both.reshape(count, -1, lanes).astype(F32)
    length = proj.shape[1]
    padded = jnp.pad(proj, ((0, 0), (2, 0), (0, 0)))
    return sum(taps[lag][:, None] * padded[:, 2 - lag : 2 - lag + length] for lag in range(3))


def convolve_plainly(mixed, skip, filters):
    near, collect, emit = filters
    keep = collect[:, 0] * collect[:, CHUNK - 2]
    groups = near.shape[0]
    length, lanes = mixed.shape[1:]
    gated = lax.optimization_barrier((mixed[0] * mixed[1]).astype(BF16)).astype(F32)
    chunks = length // CHUNK
    columns = gated.reshape(chunks, CHUNK, groups, GROUP)
    high = lax.Precision.HIGHEST
    out = jnp.einsum("gij,njgc->nigc", near, columns, precision=high)
    fresh = jnp.einsum("grj,njgc->ngrc", collect.reshape(groups, -1, CHUNK), columns, precision=high)
    state, states = jnp.zeros_like(fresh[0]), []
    for n in range(chunks):
        states.append(state)
        state = keep.reshape(groups, -1, 1) * state + fresh[n]
    out += jnp.einsum("igr,ngrc->nigc", emit.reshape(CHUNK, groups, -1), jnp.stack(states), precision=high)
    return out.reshape(length, lanes) + skip * gated


def collect_kernel(planes, where_ref, *refs):
    blocks, (given, out_ref) = refs[:planes], refs[planes:]
    core, z = where_ref[0], where_ref[1]
    lanes = given.shape[2]
    for u in range(planes):
        for owner, block in ((core, blocks[u][core]), (1 - core, given[u])):
            at = pl.multiple_of((owner * planes + (z ^ u)) * lanes, lanes)
            out_ref[:, pl.ds(at, lanes)] = block


def collect_columns(blocks, given, core, z, planes):
    tokens, lanes = given.shape[1:]
    if lanes % 128:
        keep = [lax.dynamic_index_in_dim(block, core, 0, keepdims=False) for block in blocks]
        pairs = [[jnp.where(core == c, keep[u], given[u]) for u in range(planes)] for c in range(2)]
        return jnp.concatenate([pick(pairs[c], z ^ k) for c in range(2) for k in range(planes)], axis=1)
    vmem = pl.BlockSpec(memory_space=pltpu.VMEM)
    return pl.pallas_call(
        lambda *refs: collect_kernel(planes, *refs),
        in_specs=[pl.BlockSpec(memory_space=pltpu.SMEM)] + [vmem] * (planes + 1),
        out_specs=vmem,
        out_shape=jax.ShapeDtypeStruct((tokens, 2 * planes * lanes), BF16),
        compiler_params=pltpu.CompilerParams(vmem_limit_bytes=8 << 20),
        cost_estimate=pl.CostEstimate(flops=0, bytes_accessed=0, transcendentals=0),
        name="collect_columns",
    )(jnp.stack([core, z]).astype(jnp.int32), *blocks, given)


def local(tokens, w_in, short_filter, decay_rate, residue, skip):
    n_ctx, n_ch = lax.axis_size("ctx"), lax.axis_size("ch")
    planes = n_ctx // 2
    ctx, me = lax.axis_index("ctx"), lax.axis_index("ch")
    z, core = ctx // 2, ctx % 2
    half = w_in.shape[2] // 2
    lanes = half // planes
    groups = lanes // GROUP

    block = core * planes + z
    mine = lambda a, count, axis: lax.dynamic_slice_in_dim(a, block * count, count, axis)
    decay = mine(decay_rate, groups, 0)
    filters = long_filters(decay, mine(residue, groups, 0) * jnp.sqrt(2.0 * decay))

    w_own = w_in.transpose(1, 0, 2)
    w_sib = swap_cores(w_own, n_ctx)
    got = trade_columns(tokens, me, n_ch)
    came = trade_planes(got, z, me, planes)
    w_own, w_sib, _ = lax.optimization_barrier((w_own, w_sib, got[-1]))
    w = stage(w_own, w_sib, z, core, planes)
    taps, direct = mine(short_filter, lanes, 2), mine(skip, lanes, 0)[None]
    came, filters, w, taps, direct = lax.optimization_barrier((came, filters, w, taps, direct))
    by_plane = [pick(came, z ^ k) for k in range(planes)]
    middle = planes // 2
    x = [jnp.concatenate(by_plane[:middle], axis=0), jnp.concatenate(by_plane[middle:], axis=0)]

    order = [[], []]

    def project_pieces(stream, xs, pieces, merged):
        xs = xs + [swap_cores(y, n_ctx) for y in xs]
        order[stream].extend([(side, s, h * middle) for side in range(2) for s, h in pieces])
        return project(xs, w, planes, merged)

    near = [to_column(x[0], 1, n_ch), to_column(x[1], 2, n_ch)]
    rest = [
        to_column(jnp.concatenate([x[1], near[1]], axis=0), 1, n_ch),
        to_column(jnp.concatenate([x[0], near[0]], axis=0), 2, n_ch),
    ]
    rest += [to_column(x[h], s, n_ch) for s in range(4, n_ch) for h in range(2)]
    a, b = LineSum(planes), LineSum(planes)
    blocks = project_pieces(0, x, [(0, 0), (0, 1)], True)
    a.take_and_send(blocks)
    near = tie(blocks[0], near)
    blocks = project_pieces(0, near, [(1, 0), (2, 1)], True)
    a.take_and_send(blocks)
    rest = tie(blocks[0], rest)
    halves = [(1, 1), (3, 1), (2, 0), (3, 0)] + [(s, h) for s in range(4, n_ch) for h in range(2)]
    b.take(project_pieces(1, rest, halves, False))
    for t in range(planes - 2):
        for stream in (a, b):
            stream.send_even(t)
            stream.send_odd(t)
    pair, query = finish([a, b], [slice(1, 3), slice(0, 1)])
    where = jnp.stack([core, me, z]).astype(jnp.int32)
    long_out = convolve(pair, order, taps, direct, filters, where, planes, n_ch)
    outs = gate(query, order, taps, long_out, where, planes, n_ch)
    came = [to_plane(block, u, planes) if u else block for u, block in enumerate(outs)]
    given = jnp.stack([lax.dynamic_index_in_dim(block, 1 - core, 0, keepdims=False) for block in came])
    return collect_columns(came, swap_cores(given, n_ctx), core, z, planes)


def solution(mesh):
    return jax.shard_map(
        local,
        mesh=mesh,
        in_specs=(
            P("ctx", "ch"),
            P("ctx", None, "ch"),
            P(None, None, "ch"),
            P("ch", None),
            P("ch", None),
            P("ch"),
        ),
        out_specs=P("ctx", "ch"),
        check_vma=False,
    )
```

```python
import jax
import jax.numpy as jnp
from jax import lax
from jax.experimental import pallas as pl
from jax.experimental.pallas import tpu as pltpu
from jax.sharding import PartitionSpec as P

GROUP = 16
CHUNK = 128
F32 = jnp.float32
BF16 = jnp.bfloat16


def pick(blocks, index):
    chosen = blocks[0]
    for i in range(1, len(blocks)):
        chosen = jnp.where(index == i, blocks[i], chosen)
    return chosen


def swap_cores(block, n_ctx):
    return lax.ppermute(block, "ctx", [(i, i ^ 1) for i in range(n_ctx)])


def to_plane(block, distance, planes):
    route = [(2 * z + c, 2 * (z ^ distance) + c) for z in range(planes) for c in range(2)]
    return lax.ppermute(block, "ctx", route)


def to_column(block, distance, n_ch):
    return lax.ppermute(block, "ch", [(j, j ^ distance) for j in range(n_ch)])


def trade_columns(tokens, me, n_ch):
    rows = tokens.shape[0] // n_ch
    pieces = tokens.reshape(n_ch, rows, tokens.shape[1])
    got = []
    for s in range(n_ch):
        piece = lax.dynamic_index_in_dim(pieces, me ^ s, 0, keepdims=False)
        got.append(to_column(piece, s, n_ch) if s else piece)
    return got


def trade_planes(got, z, me, planes):
    came = []
    for u in range(planes):
        piece = pick(got, me ^ z ^ u)
        came.append(to_plane(piece, u, planes) if u else piece)
    return came


def plane_of(z, r, planes):
    return (z + (1 - 2 * (z % 2)) * r + planes) % planes


def sending_order(planes):
    return [*reversed(range(planes))]


def stage_kernel(planes, where_ref, w_own, w_sib, out_ref, sems):
    z, core = where_ref[0], where_ref[1]
    depth, half = w_own.shape[1], w_own.shape[2] // 2
    lanes = half // planes
    copies = []
    for side, w in enumerate((w_own, w_sib)):
        owner = core if side == 0 else 1 - core
        rows = pl.ds(pl.multiple_of(owner * depth, depth), depth)
        for i, r in enumerate(sending_order(planes)):
            columns = pl.ds(pl.multiple_of(core * half + plane_of(z, r, planes) * lanes, lanes), lanes)
            copy = pltpu.make_async_copy(
                w.at[:, :, columns], out_ref.at[:, rows, pl.ds(i * lanes, lanes)], sems.at[side, i]
            )
            copy.start()
            copies.append(copy)
    for copy in copies:
        copy.wait()


def stage(w_own, w_sib, z, core, planes):
    depth, half = w_own.shape[1], w_own.shape[2] // 2
    lanes = half // planes
    if lanes % 128:
        w = jnp.concatenate([pick([w_own, w_sib], core), pick([w_own, w_sib], 1 - core)], axis=1)
        w = lax.dynamic_slice_in_dim(w, core * half, half, 2).reshape(3, 2 * depth, planes, lanes)
        blocks = [lax.dynamic_index_in_dim(w, plane_of(z, r, planes), 2, keepdims=False) for r in sending_order(planes)]
        return jnp.concatenate(blocks, axis=2)
    hbm = pl.BlockSpec(memory_space=pltpu.HBM)
    return pl.pallas_call(
        lambda *refs: stage_kernel(planes, *refs),
        in_specs=[pl.BlockSpec(memory_space=pltpu.SMEM), hbm, hbm],
        out_specs=pl.BlockSpec(memory_space=pltpu.VMEM),
        out_shape=jax.ShapeDtypeStruct((3, 2 * depth, half), BF16),
        scratch_shapes=[pltpu.SemaphoreType.DMA((2, planes))],
        compiler_params=pltpu.CompilerParams(vmem_limit_bytes=8 << 20),
        cost_estimate=pl.CostEstimate(flops=0, bytes_accessed=0, transcendentals=0),
        name="stage",
    )(jnp.stack([z, core]).astype(jnp.int32), w_own, w_sib)


def project_kernel(planes, pieces, merged, pairs, *refs):
    x_refs, w_ref, outs, x_all = refs[:pieces], refs[pieces], refs[pieces + 1 : -1], refs[-1]
    lanes = w_ref.shape[2] // planes
    if merged:
        outs = [outs[0].at[1], outs[0].at[0]]
    at = 0
    for ref in x_refs:
        x_all[at : at + ref.shape[0]] = ref[...]
        at += ref.shape[0]
    order = sending_order(planes)
    first = order[pairs[-1] + 1]
    for i in pairs:

        @pl.loop(0, 3)
        def _(j):
            w = w_ref[j, :, i * lanes : (i + 2) * lanes]
            sums = jnp.dot(x_all[...], w, preferred_element_type=F32).astype(BF16)
            outs[order[i] - first][j] = sums[:, :lanes]
            outs[order[i + 1] - first][j] = sums[:, lanes:]


def project(xs, w, planes, merged):
    rows = sum(x.shape[0] for x in xs)
    wide, half = w.shape[1:]
    lanes = half // planes
    if lanes % 128:
        x = jnp.concatenate(xs, axis=0)
        sums = jnp.einsum("tk,jkc->jtc", x, w, preferred_element_type=F32).astype(BF16)
        order = sending_order(planes)
        blocks = [sums[:, :, order.index(r) * lanes : (order.index(r) + 1) * lanes] for r in range(planes)]
        return [*blocks[:-2], jnp.stack([blocks[-1], blocks[-2]])] if merged else blocks
    vmem = pl.BlockSpec(memory_space=pltpu.VMEM)
    block = jax.ShapeDtypeStruct((3, rows, lanes), BF16)

    def call(merged, pairs):
        out_shape = [block] * (2 * len(pairs))
        if merged:
            out_shape = [jax.ShapeDtypeStruct((2, 3, rows, lanes), BF16)]
        return pl.pallas_call(
            lambda *refs: project_kernel(planes, len(xs), merged, pairs, *refs),
            in_specs=[vmem] * (len(xs) + 1),
            out_specs=[vmem] * len(out_shape),
            out_shape=out_shape,
            scratch_shapes=[pltpu.VMEM((rows, wide), BF16)],
            compiler_params=pltpu.CompilerParams(vmem_limit_bytes=8 << 20),
            cost_estimate=pl.CostEstimate(flops=0, bytes_accessed=0, transcendentals=0),
            name="project",
        )(*xs, pltpu.with_memory_space_constraint(w, pltpu.VMEM))

    pairs = [*range(0, planes, 2)]
    return [*call(False, pairs[1:]), *call(True, pairs[:1])] if merged else call(False, pairs)


def add(*blocks):
    total = blocks[0].astype(F32)
    for block in blocks[1:]:
        total = total + block.astype(F32)
    return total.astype(BF16)


class LineSum:
    def __init__(self, planes):
        self.planes, self.last = planes, planes - 1
        self.blocks = [[] for _ in range(planes)]
        self.even, self.odd = {-1: []}, {-1: []}

    def take(self, blocks):
        for mine, block in zip(self.blocks, blocks, strict=True):
            mine.append(block)

    def take_and_send(self, blocks):
        *blocks, first = blocks
        self.take([*blocks, first[1], first[0]])
        came = self.exchange(0, first, 0)
        for t in range(2):
            self.even.setdefault(t, []).append(came[t])
        self.odd[0] = []

    def exchange(self, t, block, first):
        route = []
        for e in range(first, self.last, 2):
            if e <= t:
                route += [(2 * e + c, 2 * e + 2 + c) for c in range(2)]
            if self.last - e - 1 <= t:
                route += [(2 * e + 2 + c, 2 * e + c) for c in range(2)]
        return lax.ppermute(block, "ctx", route) if route else None

    def send(self, t, r, came, first):
        sent = self.exchange(t, add_parts(self.blocks[r], came), first)
        return [] if sent is None else [sent]

    def send_even(self, t):
        if t not in self.even:
            self.even[t] = self.send(t, self.last - t, self.odd[t - 1], 0)

    def send_odd(self, t):
        if t not in self.odd:
            self.odd[t] = self.send(t, t + 1, self.even[t - 1], 1)


def finish(streams, cuts):
    last = streams[0].last
    t = last - 1
    for stream in streams:
        stream.send_even(t)
    odd = [add_parts(stream.blocks[t + 1], stream.even[t - 1]) for stream in streams]
    whole = lambda value: jnp.concatenate(value, axis=1) if len(value) > 1 else value[0]
    near = [(whole(stream.blocks[0]), whole(stream.even[t])) for stream in streams]
    terms = []
    for cut in cuts:
        came = streams[0].exchange(t, jnp.concatenate([block[cut] for block in odd], axis=1), 1)
        row, of_cut = 0, []
        for block, even in near:
            of_cut.append([(block, cut.start, 0), (even, cut.start, 0), (came, 0, row)])
            row += block.shape[1]
        terms.append(of_cut)
    return terms


def add_parts(*values):
    values = [value for value in values if value]
    if len({len(value) for value in values}) > 1:
        values = [[jnp.concatenate(value, axis=1)] if len(value) > 1 else value for value in values]
    parts = [add(*blocks) if len(blocks) > 1 else blocks[0] for blocks in zip(*values, strict=True)]
    return jnp.concatenate(parts, axis=1) if len(parts) > 1 else parts[0]


def tie(first, then):
    return lax.optimization_barrier((first, then))[1]


def long_filters(decay, weight):
    lag = jnp.arange(CHUNK)
    apart = lag[:, None] - lag[None, :]
    away = jnp.maximum(apart, 0).astype(F32)
    near = jnp.sum(
        weight[:, :, None, None] * jnp.exp(-decay[:, :, None, None] * away[None, None]), axis=1
    )
    near = jnp.where(apart[None] >= 0, near, 0.0)
    poles = decay.reshape(-1)
    position = lag.astype(F32)
    collect = jnp.exp(-poles[:, None] * (CHUNK - 1 - position)[None, :])
    emit = weight.reshape(-1)[None, :] * jnp.exp(-poles[None, :] * (position + 1.0)[:, None])
    return near, collect, emit


def halves_of(value):
    high = value.astype(BF16)
    return high, (value - high.astype(F32)).astype(BF16)


def unpack(data):
    arrays, places = [], []
    for terms in data:
        places.append([])
        for array, plane, row in terms:
            at = next((i for i, known in enumerate(arrays) if known is array), len(arrays))
            arrays += [array] if at == len(arrays) else []
            places[-1].append((at, plane, row))
    return arrays, places


def place(order, data, refs, count, proj, where_ref, planes, n_ch):
    core, me = where_ref[0], where_ref[1]
    proj[:, 0:8] = jnp.zeros((count, 8, proj.shape[2]), F32)
    rows = CHUNK // n_ch
    for pieces, terms in zip(order, data, strict=True):
        start = 0
        for side, s, k0 in pieces:
            owner = core if side == 0 else 1 - core
            for k in range(k0, k0 + planes // 2):
                at = pl.multiple_of((2 * k + owner) * CHUNK + (me ^ s) * rows + 8, 8)
                for j in range(count):
                    total = add(*(refs[i][plane + j, row + start : row + start + rows] for i, plane, row in terms))
                    proj[j, pl.ds(at, rows)] = total.astype(F32)
                start += rows


def short_mix(taps, j, proj, at, n):
    total = 0.0
    for lag in range(3):
        total += taps[lag, j : j + 1] * proj[at, 8 - lag + n * CHUNK : 8 - lag + (n + 1) * CHUNK]
    return total


def convolve_kernel(order, data, count, planes, n_ch, where_ref, *refs):
    taps, skip, near, collect, emit, done, proj, long_in = refs[count:]
    lanes = skip.shape[1]
    groups = near.shape[0]
    place(order, data, refs, 2, proj, where_ref, planes, n_ch)

    lane_group = lax.broadcasted_iota(jnp.int32, (1, lanes), 1) // GROUP
    pole_group = lax.broadcasted_iota(jnp.int32, (collect.shape[0], lanes), 0) // (collect.shape[0] // groups)
    same = pole_group == lane_group
    keep = collect[:, 0:1] * collect[:, CHUNK - 2 : CHUNK - 1]
    collect2 = jnp.concatenate(halves_of(collect[...]), axis=1)
    emit_high, emit_low = halves_of(emit[...])
    emit3 = jnp.concatenate([emit_high, emit_low, emit_high], axis=1)
    state = jnp.zeros(same.shape, F32)
    chunks = 2 * planes
    for n in range(chunks):
        gated = (short_mix(taps, 1, proj, 0, n) * short_mix(taps, 2, proj, 1, n)).astype(BF16)
        gated2 = jnp.concatenate([gated, gated], axis=0)
        long_out = skip[...] * gated.astype(F32)
        if n:
            state_high, state_low = halves_of(state)
            long_out += jnp.dot(
                emit3, jnp.concatenate([state_high, state_high, state_low], axis=0), preferred_element_type=F32
            )
        if n < chunks - 1:
            fresh = jnp.dot(collect2, gated2, preferred_element_type=F32)
            state = keep * state + jnp.where(same, fresh, 0.0)
        long_in[n // 2, n % 2] = gated2
        done[n * CHUNK : (n + 1) * CHUNK] = long_out
    for g in range(groups):
        near2 = jnp.concatenate(halves_of(near[g]), axis=1)
        mine = lane_group == g
        for k in range(planes):
            pair = jnp.concatenate([long_in[k, 0], long_in[k, 1]], axis=1)
            both = jnp.dot(near2, pair, preferred_element_type=F32)
            for c in range(2):
                at = slice((2 * k + c) * CHUNK, (2 * k + c + 1) * CHUNK)
                done[at] += jnp.where(mine, both[:, c * lanes : (c + 1) * lanes], 0.0)


def convolve(data, order, taps, skip, filters, where, planes, n_ch):
    lanes = skip.shape[1]
    length = 2 * planes * CHUNK
    if lanes % 128:
        mixed = mix_plainly(data, order, 2, taps[:, 1:], where, planes, n_ch)
        return convolve_plainly(mixed, skip, filters)
    vmem = pl.BlockSpec(memory_space=pltpu.VMEM)
    arrays, data = unpack(data)
    return pl.pallas_call(
        lambda *refs: convolve_kernel(order, data, len(arrays), planes, n_ch, *refs),
        in_specs=[pl.BlockSpec(memory_space=pltpu.SMEM)] + [vmem] * (len(arrays) + 5),
        out_specs=vmem,
        out_shape=jax.ShapeDtypeStruct((length, lanes), F32),
        scratch_shapes=[
            pltpu.VMEM((2, length + 8, lanes), F32),
            pltpu.VMEM((planes, 2, 2 * CHUNK, lanes), BF16),
        ],
        compiler_params=pltpu.CompilerParams(vmem_limit_bytes=8 << 20),
        cost_estimate=pl.CostEstimate(flops=0, bytes_accessed=0, transcendentals=0),
        name="convolve",
    )(where, *arrays, taps, skip, *filters)


def gate_kernel(order, data, count, planes, n_ch, where_ref, *refs):
    taps, long_out = refs[count : count + 2]
    outs, (proj, done) = refs[count + 2 : -2], refs[-2:]
    z = where_ref[2]
    place(order, data, refs, 1, proj, where_ref, planes, n_ch)
    for n in range(2 * planes):
        at = slice(n * CHUNK, (n + 1) * CHUNK)
        done[at] = (short_mix(taps, 0, proj, 0, n) * long_out[at]).astype(BF16)
    for u in range(planes):
        at = pl.multiple_of((z ^ u) * 2 * CHUNK, CHUNK)
        outs[u][...] = done[pl.ds(at, 2 * CHUNK)].reshape(outs[u].shape)


def gate(data, order, taps, long_out, where, planes, n_ch):
    length, lanes = long_out.shape
    if lanes % 128:
        mixed = mix_plainly(data, order, 1, taps[:, :1], where, planes, n_ch)
        out = (mixed[0] * long_out).astype(BF16).reshape(planes, 2, CHUNK, lanes)
        return [lax.dynamic_index_in_dim(out, where[2] ^ u, 0, keepdims=False) for u in range(planes)]
    vmem = pl.BlockSpec(memory_space=pltpu.VMEM)
    arrays, data = unpack(data)
    return pl.pallas_call(
        lambda *refs: gate_kernel(order, data, len(arrays), planes, n_ch, *refs),
        in_specs=[pl.BlockSpec(memory_space=pltpu.SMEM)] + [vmem] * (len(arrays) + 2),
        out_specs=[vmem] * planes,
        out_shape=[jax.ShapeDtypeStruct((2, CHUNK, lanes), BF16)] * planes,
        scratch_shapes=[pltpu.VMEM((1, length + 8, lanes), F32), pltpu.VMEM((length, lanes), BF16)],
        compiler_params=pltpu.CompilerParams(vmem_limit_bytes=8 << 20),
        cost_estimate=pl.CostEstimate(flops=0, bytes_accessed=0, transcendentals=0),
        name="gate",
    )(where, *arrays, taps, long_out)


def mix_plainly(data, order, count, taps, where, planes, n_ch):
    core, me = where[0], where[1]
    lanes = taps.shape[2]
    length = [terms[0][0].shape[1] for terms in data]
    data = [
        add(*(array[plane : plane + count, row : row + rows] for array, plane, row in terms))
        for terms, rows in zip(data, length, strict=True)
    ]
    rows = CHUNK // n_ch
    sides = [[[None, None] for _ in range(n_ch)] for _ in range(2)]
    for pieces, block in zip(order, data, strict=True):
        cut = block.reshape(count, len(pieces), planes // 2, rows, lanes)
        for i, (side, s, first) in enumerate(pieces):
            sides[side][s][first > 0] = cut[:, i]
    sides = [[jnp.concatenate(halves, axis=1) for halves in side] for side in sides]
    sides = [jnp.stack([pick(side, me ^ p) for p in range(n_ch)], axis=2) for side in sides]
    both = jnp.stack([pick(sides, core), pick(sides, 1 - core)], axis=2)
    proj = both.reshape(count, -1, lanes).astype(F32)
    length = proj.shape[1]
    padded = jnp.pad(proj, ((0, 0), (2, 0), (0, 0)))
    return sum(taps[lag][:, None] * padded[:, 2 - lag : 2 - lag + length] for lag in range(3))


def convolve_plainly(mixed, skip, filters):
    near, collect, emit = filters
    keep = collect[:, 0] * collect[:, CHUNK - 2]
    groups = near.shape[0]
    length, lanes = mixed.shape[1:]
    gated = lax.optimization_barrier((mixed[0] * mixed[1]).astype(BF16)).astype(F32)
    chunks = length // CHUNK
    columns = gated.reshape(chunks, CHUNK, groups, GROUP)
    high = lax.Precision.HIGHEST
    out = jnp.einsum("gij,njgc->nigc", near, columns, precision=high)
    fresh = jnp.einsum("grj,njgc->ngrc", collect.reshape(groups, -1, CHUNK), columns, precision=high)
    state, states = jnp.zeros_like(fresh[0]), []
    for n in range(chunks):
        states.append(state)
        state = keep.reshape(groups, -1, 1) * state + fresh[n]
    out += jnp.einsum("igr,ngrc->nigc", emit.reshape(CHUNK, groups, -1), jnp.stack(states), precision=high)
    return out.reshape(length, lanes) + skip * gated


def collect_kernel(planes, where_ref, *refs):
    blocks, (given, out_ref) = refs[:planes], refs[planes:]
    core, z = where_ref[0], where_ref[1]
    lanes = given.shape[2]
    for u in range(planes):
        for owner, block in ((core, blocks[u][core]), (1 - core, given[u])):
            at = pl.multiple_of((owner * planes + (z ^ u)) * lanes, lanes)
            out_ref[:, pl.ds(at, lanes)] = block


def collect_columns(blocks, given, core, z, planes):
    tokens, lanes = given.shape[1:]
    if lanes % 128:
        keep = [lax.dynamic_index_in_dim(block, core, 0, keepdims=False) for block in blocks]
        pairs = [[jnp.where(core == c, keep[u], given[u]) for u in range(planes)] for c in range(2)]
        return jnp.concatenate([pick(pairs[c], z ^ k) for c in range(2) for k in range(planes)], axis=1)
    vmem = pl.BlockSpec(memory_space=pltpu.VMEM)
    return pl.pallas_call(
        lambda *refs: collect_kernel(planes, *refs),
        in_specs=[pl.BlockSpec(memory_space=pltpu.SMEM)] + [vmem] * (planes + 1),
        out_specs=vmem,
        out_shape=jax.ShapeDtypeStruct((tokens, 2 * planes * lanes), BF16),
        compiler_params=pltpu.CompilerParams(vmem_limit_bytes=8 << 20),
        cost_estimate=pl.CostEstimate(flops=0, bytes_accessed=0, transcendentals=0),
        name="collect_columns",
    )(jnp.stack([core, z]).astype(jnp.int32), *blocks, given)


def local(tokens, w_in, short_filter, decay_rate, residue, skip):
    n_ctx, n_ch = lax.axis_size("ctx"), lax.axis_size("ch")
    planes = n_ctx // 2
    ctx, me = lax.axis_index("ctx"), lax.axis_index("ch")
    z, core = ctx // 2, ctx % 2
    half = w_in.shape[2] // 2
    lanes = half // planes
    groups = lanes // GROUP

    block = core * planes + z
    mine = lambda a, count, axis: lax.dynamic_slice_in_dim(a, block * count, count, axis)
    decay = mine(decay_rate, groups, 0)
    filters = long_filters(decay, mine(residue, groups, 0) * jnp.sqrt(2.0 * decay))

    w_own = w_in.transpose(1, 0, 2)
    w_sib = swap_cores(w_own, n_ctx)
    got = trade_columns(tokens, me, n_ch)
    came = trade_planes(got, z, me, planes)
    w_own, w_sib, _ = lax.optimization_barrier((w_own, w_sib, got[-1]))
    w = stage(w_own, w_sib, z, core, planes)
    taps, direct = mine(short_filter, lanes, 2), mine(skip, lanes, 0)[None]
    came, filters, w, taps, direct = lax.optimization_barrier((came, filters, w, taps, direct))
    by_plane = [pick(came, z ^ k) for k in range(planes)]
    middle = planes // 2
    x = [jnp.concatenate(by_plane[:middle], axis=0), jnp.concatenate(by_plane[middle:], axis=0)]

    order = [[], []]

    def project_pieces(stream, xs, pieces, merged):
        xs = xs + [swap_cores(y, n_ctx) for y in xs]
        order[stream].extend([(side, s, h * middle) for side in range(2) for s, h in pieces])
        return project(xs, w, planes, merged)

    near = [to_column(x[0], 1, n_ch), to_column(x[1], 2, n_ch)]
    rest = [
        to_column(jnp.concatenate([x[1], near[1]], axis=0), 1, n_ch),
        to_column(jnp.concatenate([x[0], near[0]], axis=0), 2, n_ch),
    ]
    rest += [to_column(x[h], s, n_ch) for s in range(4, n_ch) for h in range(2)]
    a, b = LineSum(planes), LineSum(planes)
    blocks = project_pieces(0, x, [(0, 0), (0, 1)], True)
    a.take_and_send(blocks)
    near = tie(blocks[-1], near)
    blocks = project_pieces(0, near, [(1, 0), (2, 1)], True)
    a.take_and_send(blocks)
    rest = tie(blocks[-1], rest)
    halves = [(1, 1), (3, 1), (2, 0), (3, 0)] + [(s, h) for s in range(4, n_ch) for h in range(2)]
    b.take(project_pieces(1, rest, halves, False))
    for t in range(planes - 2):
        for stream in (a, b):
            stream.send_even(t)
            stream.send_odd(t)
    pair, query = finish([a, b], [slice(1, 3), slice(0, 1)])
    where = jnp.stack([core, me, z]).astype(jnp.int32)
    long_out = convolve(pair, order, taps, direct, filters, where, planes, n_ch)
    outs = gate(query, order, taps, long_out, where, planes, n_ch)
    came = [to_plane(block, u, planes) if u else block for u, block in enumerate(outs)]
    given = jnp.stack([lax.dynamic_index_in_dim(block, 1 - core, 0, keepdims=False) for block in came])
    return collect_columns(came, swap_cores(given, n_ctx), core, z, planes)


def solution(mesh):
    return jax.shard_map(
        local,
        mesh=mesh,
        in_specs=(
            P("ctx", "ch"),
            P("ctx", None, "ch"),
            P(None, None, "ch"),
            P("ch", None),
            P("ch", None),
            P("ch"),
        ),
        out_specs=P("ctx", "ch"),
        check_vma=False,
    )
```

```python
import jax
import jax.numpy as jnp
from jax import lax
from jax.experimental import pallas as pl
from jax.experimental.pallas import tpu as pltpu
from jax.sharding import PartitionSpec as P

GROUP = 16
CHUNK = 128
F32 = jnp.float32
BF16 = jnp.bfloat16


def pick(blocks, index):
    chosen = blocks[0]
    for i in range(1, len(blocks)):
        chosen = jnp.where(index == i, blocks[i], chosen)
    return chosen


def swap_cores(block, n_ctx):
    return lax.ppermute(block, "ctx", [(i, i ^ 1) for i in range(n_ctx)])


def to_plane(block, distance, planes):
    route = [(2 * z + c, 2 * (z ^ distance) + c) for z in range(planes) for c in range(2)]
    return lax.ppermute(block, "ctx", route)


def to_column(block, distance, n_ch):
    return lax.ppermute(block, "ch", [(j, j ^ distance) for j in range(n_ch)])


def trade_columns(tokens, me, n_ch):
    rows = tokens.shape[0] // n_ch
    pieces = tokens.reshape(n_ch, rows, tokens.shape[1])
    got = []
    for s in range(n_ch):
        piece = lax.dynamic_index_in_dim(pieces, me ^ s, 0, keepdims=False)
        got.append(to_column(piece, s, n_ch) if s else piece)
    return got


def trade_planes(got, z, me, planes):
    came = []
    for u in range(planes):
        piece = pick(got, me ^ z ^ u)
        came.append(to_plane(piece, u, planes) if u else piece)
    return came


def plane_of(z, r, planes):
    return (z + (1 - 2 * (z % 2)) * r + planes) % planes


def sending_order(planes):
    return [*reversed(range(planes))]


def stage_kernel(planes, where_ref, w_own, w_sib, out_ref, sems):
    z, core = where_ref[0], where_ref[1]
    depth, half = w_own.shape[1], w_own.shape[2] // 2
    lanes = half // planes
    copies = []
    for side, w in enumerate((w_own, w_sib)):
        owner = core if side == 0 else 1 - core
        rows = pl.ds(pl.multiple_of(owner * depth, depth), depth)
        for i, r in enumerate(sending_order(planes)):
            columns = pl.ds(pl.multiple_of(core * half + plane_of(z, r, planes) * lanes, lanes), lanes)
            copy = pltpu.make_async_copy(
                w.at[:, :, columns], out_ref.at[:, rows, pl.ds(i * lanes, lanes)], sems.at[side, i]
            )
            copy.start()
            copies.append(copy)
    for copy in copies:
        copy.wait()


def stage(w_own, w_sib, z, core, planes):
    depth, half = w_own.shape[1], w_own.shape[2] // 2
    lanes = half // planes
    if lanes % 128:
        w = jnp.concatenate([pick([w_own, w_sib], core), pick([w_own, w_sib], 1 - core)], axis=1)
        w = lax.dynamic_slice_in_dim(w, core * half, half, 2).reshape(3, 2 * depth, planes, lanes)
        blocks = [lax.dynamic_index_in_dim(w, plane_of(z, r, planes), 2, keepdims=False) for r in sending_order(planes)]
        return jnp.concatenate(blocks, axis=2)
    hbm = pl.BlockSpec(memory_space=pltpu.HBM)
    return pl.pallas_call(
        lambda *refs: stage_kernel(planes, *refs),
        in_specs=[pl.BlockSpec(memory_space=pltpu.SMEM), hbm, hbm],
        out_specs=pl.BlockSpec(memory_space=pltpu.VMEM),
        out_shape=jax.ShapeDtypeStruct((3, 2 * depth, half), BF16),
        scratch_shapes=[pltpu.SemaphoreType.DMA((2, planes))],
        compiler_params=pltpu.CompilerParams(vmem_limit_bytes=8 << 20),
        cost_estimate=pl.CostEstimate(flops=0, bytes_accessed=0, transcendentals=0),
        name="stage",
    )(jnp.stack([z, core]).astype(jnp.int32), w_own, w_sib)


def project_kernel(planes, pieces, merged, pairs, *refs):
    x_refs, w_ref, outs, x_all = refs[:pieces], refs[pieces], refs[pieces + 1 : -1], refs[-1]
    lanes = w_ref.shape[2] // planes
    if merged:
        outs = [outs[0].at[1], outs[0].at[0]]
    at = 0
    for ref in x_refs:
        x_all[at : at + ref.shape[0]] = ref[...]
        at += ref.shape[0]
    order = sending_order(planes)
    first = order[pairs[-1] + 1]
    for i in pairs:

        @pl.loop(0, 3)
        def _(j):
            w = w_ref[j, :, i * lanes : (i + 2) * lanes]
            sums = jnp.dot(x_all[...], w, preferred_element_type=F32).astype(BF16)
            outs[order[i] - first][j] = sums[:, :lanes]
            outs[order[i + 1] - first][j] = sums[:, lanes:]


def project(xs, w, planes, merged):
    rows = sum(x.shape[0] for x in xs)
    wide, half = w.shape[1:]
    lanes = half // planes
    if lanes % 128:
        x = jnp.concatenate(xs, axis=0)
        sums = jnp.einsum("tk,jkc->jtc", x, w, preferred_element_type=F32).astype(BF16)
        order = sending_order(planes)
        blocks = [sums[:, :, order.index(r) * lanes : (order.index(r) + 1) * lanes] for r in range(planes)]
        return [*blocks[:-2], jnp.stack([blocks[-1], blocks[-2]])] if merged else blocks
    vmem = pl.BlockSpec(memory_space=pltpu.VMEM)
    block = jax.ShapeDtypeStruct((3, rows, lanes), BF16)

    def call(merged, pairs):
        out_shape = [block] * (2 * len(pairs))
        if merged:
            out_shape = [jax.ShapeDtypeStruct((2, 3, rows, lanes), BF16)]
        return pl.pallas_call(
            lambda *refs: project_kernel(planes, len(xs), merged, pairs, *refs),
            in_specs=[vmem] * (len(xs) + 1),
            out_specs=[vmem] * len(out_shape),
            out_shape=out_shape,
            scratch_shapes=[pltpu.VMEM((rows, wide), BF16)],
            compiler_params=pltpu.CompilerParams(vmem_limit_bytes=8 << 20),
            cost_estimate=pl.CostEstimate(flops=0, bytes_accessed=0, transcendentals=0),
            name="project",
        )(*xs, pltpu.with_memory_space_constraint(w, pltpu.VMEM))

    pairs = [*range(0, planes, 2)]
    return [*call(False, pairs[1:]), *call(merged, pairs[:1])]


def add(*blocks):
    total = blocks[0].astype(F32)
    for block in blocks[1:]:
        total = total + block.astype(F32)
    return total.astype(BF16)


class LineSum:
    def __init__(self, planes):
        self.planes, self.last = planes, planes - 1
        self.blocks = [[] for _ in range(planes)]
        self.even, self.odd = {-1: []}, {-1: []}

    def take(self, blocks):
        for mine, block in zip(self.blocks, blocks, strict=True):
            mine.append(block)

    def take_and_send(self, blocks):
        *blocks, first = blocks
        self.take([*blocks, first[1], first[0]])
        came = self.exchange(0, first, 0)
        for t in range(2):
            self.even.setdefault(t, []).append(came[t])
        self.odd[0] = []

    def exchange(self, t, block, first):
        route = []
        for e in range(first, self.last, 2):
            if e <= t:
                route += [(2 * e + c, 2 * e + 2 + c) for c in range(2)]
            if self.last - e - 1 <= t:
                route += [(2 * e + 2 + c, 2 * e + c) for c in range(2)]
        return lax.ppermute(block, "ctx", route) if route else None

    def send(self, t, r, came, first):
        sent = self.exchange(t, add_parts(self.blocks[r], came), first)
        return [] if sent is None else [sent]

    def send_even(self, t):
        if t not in self.even:
            self.even[t] = self.send(t, self.last - t, self.odd[t - 1], 0)

    def send_odd(self, t):
        if t not in self.odd:
            self.odd[t] = self.send(t, t + 1, self.even[t - 1], 1)


def finish(streams, cuts):
    last = streams[0].last
    t = last - 1
    for stream in streams:
        stream.send_even(t)
    odd = [add_parts(stream.blocks[t + 1], stream.even[t - 1]) for stream in streams]
    whole = lambda value: jnp.concatenate(value, axis=1) if len(value) > 1 else value[0]
    near = [(whole(stream.blocks[0]), whole(stream.even[t])) for stream in streams]
    terms = []
    for cut in cuts:
        came = streams[0].exchange(t, jnp.concatenate([block[cut] for block in odd], axis=1), 1)
        row, of_cut = 0, []
        for block, even in near:
            of_cut.append([(block, cut.start, 0), (even, cut.start, 0), (came, 0, row)])
            row += block.shape[1]
        terms.append(of_cut)
    return terms


def add_parts(*values):
    values = [value for value in values if value]
    if len({len(value) for value in values}) > 1:
        values = [[jnp.concatenate(value, axis=1)] if len(value) > 1 else value for value in values]
    parts = [add(*blocks) if len(blocks) > 1 else blocks[0] for blocks in zip(*values, strict=True)]
    return jnp.concatenate(parts, axis=1) if len(parts) > 1 else parts[0]


def tie(first, then):
    return lax.optimization_barrier((first, then))[1]


def long_filters(decay, weight):
    lag = jnp.arange(CHUNK)
    apart = lag[:, None] - lag[None, :]
    away = jnp.maximum(apart, 0).astype(F32)
    near = jnp.sum(
        weight[:, :, None, None] * jnp.exp(-decay[:, :, None, None] * away[None, None]), axis=1
    )
    near = jnp.where(apart[None] >= 0, near, 0.0)
    poles = decay.reshape(-1)
    position = lag.astype(F32)
    collect = jnp.exp(-poles[:, None] * (CHUNK - 1 - position)[None, :])
    emit = weight.reshape(-1)[None, :] * jnp.exp(-poles[None, :] * (position + 1.0)[:, None])
    return near, collect, emit


def halves_of(value):
    high = value.astype(BF16)
    return high, (value - high.astype(F32)).astype(BF16)


def unpack(data):
    arrays, places = [], []
    for terms in data:
        places.append([])
        for array, plane, row in terms:
            at = next((i for i, known in enumerate(arrays) if known is array), len(arrays))
            arrays += [array] if at == len(arrays) else []
            places[-1].append((at, plane, row))
    return arrays, places


def place(order, data, refs, count, proj, where_ref, planes, n_ch):
    core, me = where_ref[0], where_ref[1]
    proj[:, 0:8] = jnp.zeros((count, 8, proj.shape[2]), F32)
    rows = CHUNK // n_ch
    for pieces, terms in zip(order, data, strict=True):
        start = 0
        for side, s, k0 in pieces:
            owner = core if side == 0 else 1 - core
            for k in range(k0, k0 + planes // 2):
                at = pl.multiple_of((2 * k + owner) * CHUNK + (me ^ s) * rows + 8, 8)
                for j in range(count):
                    total = add(*(refs[i][plane + j, row + start : row + start + rows] for i, plane, row in terms))
                    proj[j, pl.ds(at, rows)] = total.astype(F32)
                start += rows


def short_mix(taps, j, proj, at, n):
    total = 0.0
    for lag in range(3):
        total += taps[lag, j : j + 1] * proj[at, 8 - lag + n * CHUNK : 8 - lag + (n + 1) * CHUNK]
    return total


def convolve_kernel(order, data, count, planes, n_ch, where_ref, *refs):
    taps, skip, near, collect, emit, done, proj, long_in = refs[count:]
    lanes = skip.shape[1]
    groups = near.shape[0]
    place(order, data, refs, 2, proj, where_ref, planes, n_ch)

    lane_group = lax.broadcasted_iota(jnp.int32, (1, lanes), 1) // GROUP
    pole_group = lax.broadcasted_iota(jnp.int32, (collect.shape[0], lanes), 0) // (collect.shape[0] // groups)
    same = pole_group == lane_group
    keep = collect[:, 0:1] * collect[:, CHUNK - 2 : CHUNK - 1]
    collect2 = jnp.concatenate(halves_of(collect[...]), axis=1)
    emit_high, emit_low = halves_of(emit[...])
    emit3 = jnp.concatenate([emit_high, emit_low, emit_high], axis=1)
    state = jnp.zeros(same.shape, F32)
    chunks = 2 * planes
    for n in range(chunks):
        gated = (short_mix(taps, 1, proj, 0, n) * short_mix(taps, 2, proj, 1, n)).astype(BF16)
        gated2 = jnp.concatenate([gated, gated], axis=0)
        long_out = skip[...] * gated.astype(F32)
        if n:
            state_high, state_low = halves_of(state)
            long_out += jnp.dot(
                emit3, jnp.concatenate([state_high, state_high, state_low], axis=0), preferred_element_type=F32
            )
        if n < chunks - 1:
            fresh = jnp.dot(collect2, gated2, preferred_element_type=F32)
            state = keep * state + jnp.where(same, fresh, 0.0)
        long_in[n // 2, n % 2] = gated2
        done[n * CHUNK : (n + 1) * CHUNK] = long_out
    for g in range(groups):
        near2 = jnp.concatenate(halves_of(near[g]), axis=1)
        mine = lane_group == g
        for k in range(planes):
            pair = jnp.concatenate([long_in[k, 0], long_in[k, 1]], axis=1)
            both = jnp.dot(near2, pair, preferred_element_type=F32)
            for c in range(2):
                at = slice((2 * k + c) * CHUNK, (2 * k + c + 1) * CHUNK)
                done[at] += jnp.where(mine, both[:, c * lanes : (c + 1) * lanes], 0.0)


def convolve(data, order, taps, skip, filters, where, planes, n_ch):
    lanes = skip.shape[1]
    length = 2 * planes * CHUNK
    if lanes % 128:
        mixed = mix_plainly(data, order, 2, taps[:, 1:], where, planes, n_ch)
        return convolve_plainly(mixed, skip, filters)
    vmem = pl.BlockSpec(memory_space=pltpu.VMEM)
    arrays, data = unpack(data)
    return pl.pallas_call(
        lambda *refs: convolve_kernel(order, data, len(arrays), planes, n_ch, *refs),
        in_specs=[pl.BlockSpec(memory_space=pltpu.SMEM)] + [vmem] * (len(arrays) + 5),
        out_specs=vmem,
        out_shape=jax.ShapeDtypeStruct((length, lanes), F32),
        scratch_shapes=[
            pltpu.VMEM((2, length + 8, lanes), F32),
            pltpu.VMEM((planes, 2, 2 * CHUNK, lanes), BF16),
        ],
        compiler_params=pltpu.CompilerParams(vmem_limit_bytes=8 << 20),
        cost_estimate=pl.CostEstimate(flops=0, bytes_accessed=0, transcendentals=0),
        name="convolve",
    )(where, *arrays, taps, skip, *filters)


def gate_kernel(order, data, count, planes, n_ch, where_ref, *refs):
    taps, long_out = refs[count : count + 2]
    outs, (proj, done) = refs[count + 2 : -2], refs[-2:]
    z = where_ref[2]
    place(order, data, refs, 1, proj, where_ref, planes, n_ch)
    for n in range(2 * planes):
        at = slice(n * CHUNK, (n + 1) * CHUNK)
        done[at] = (short_mix(taps, 0, proj, 0, n) * long_out[at]).astype(BF16)
    for u in range(planes):
        at = pl.multiple_of((z ^ u) * 2 * CHUNK, CHUNK)
        outs[u][...] = done[pl.ds(at, 2 * CHUNK)].reshape(outs[u].shape)


def gate(data, order, taps, long_out, where, planes, n_ch):
    length, lanes = long_out.shape
    if lanes % 128:
        mixed = mix_plainly(data, order, 1, taps[:, :1], where, planes, n_ch)
        out = (mixed[0] * long_out).astype(BF16).reshape(planes, 2, CHUNK, lanes)
        return [lax.dynamic_index_in_dim(out, where[2] ^ u, 0, keepdims=False) for u in range(planes)]
    vmem = pl.BlockSpec(memory_space=pltpu.VMEM)
    arrays, data = unpack(data)
    return pl.pallas_call(
        lambda *refs: gate_kernel(order, data, len(arrays), planes, n_ch, *refs),
        in_specs=[pl.BlockSpec(memory_space=pltpu.SMEM)] + [vmem] * (len(arrays) + 2),
        out_specs=[vmem] * planes,
        out_shape=[jax.ShapeDtypeStruct((2, CHUNK, lanes), BF16)] * planes,
        scratch_shapes=[pltpu.VMEM((1, length + 8, lanes), F32), pltpu.VMEM((length, lanes), BF16)],
        compiler_params=pltpu.CompilerParams(vmem_limit_bytes=8 << 20),
        cost_estimate=pl.CostEstimate(flops=0, bytes_accessed=0, transcendentals=0),
        name="gate",
    )(where, *arrays, taps, long_out)


def mix_plainly(data, order, count, taps, where, planes, n_ch):
    core, me = where[0], where[1]
    lanes = taps.shape[2]
    length = [terms[0][0].shape[1] for terms in data]
    data = [
        add(*(array[plane : plane + count, row : row + rows] for array, plane, row in terms))
        for terms, rows in zip(data, length, strict=True)
    ]
    rows = CHUNK // n_ch
    sides = [[[None, None] for _ in range(n_ch)] for _ in range(2)]
    for pieces, block in zip(order, data, strict=True):
        cut = block.reshape(count, len(pieces), planes // 2, rows, lanes)
        for i, (side, s, first) in enumerate(pieces):
            sides[side][s][first > 0] = cut[:, i]
    sides = [[jnp.concatenate(halves, axis=1) for halves in side] for side in sides]
    sides = [jnp.stack([pick(side, me ^ p) for p in range(n_ch)], axis=2) for side in sides]
    both = jnp.stack([pick(sides, core), pick(sides, 1 - core)], axis=2)
    proj = both.reshape(count, -1, lanes).astype(F32)
    length = proj.shape[1]
    padded = jnp.pad(proj, ((0, 0), (2, 0), (0, 0)))
    return sum(taps[lag][:, None] * padded[:, 2 - lag : 2 - lag + length] for lag in range(3))


def convolve_plainly(mixed, skip, filters):
    near, collect, emit = filters
    keep = collect[:, 0] * collect[:, CHUNK - 2]
    groups = near.shape[0]
    length, lanes = mixed.shape[1:]
    gated = lax.optimization_barrier((mixed[0] * mixed[1]).astype(BF16)).astype(F32)
    chunks = length // CHUNK
    columns = gated.reshape(chunks, CHUNK, groups, GROUP)
    high = lax.Precision.HIGHEST
    out = jnp.einsum("gij,njgc->nigc", near, columns, precision=high)
    fresh = jnp.einsum("grj,njgc->ngrc", collect.reshape(groups, -1, CHUNK), columns, precision=high)
    state, states = jnp.zeros_like(fresh[0]), []
    for n in range(chunks):
        states.append(state)
        state = keep.reshape(groups, -1, 1) * state + fresh[n]
    out += jnp.einsum("igr,ngrc->nigc", emit.reshape(CHUNK, groups, -1), jnp.stack(states), precision=high)
    return out.reshape(length, lanes) + skip * gated


def collect_kernel(planes, where_ref, *refs):
    blocks, (given, out_ref) = refs[:planes], refs[planes:]
    core, z = where_ref[0], where_ref[1]
    lanes = given.shape[2]
    for u in range(planes):
        for owner, block in ((core, blocks[u][core]), (1 - core, given[u])):
            at = pl.multiple_of((owner * planes + (z ^ u)) * lanes, lanes)
            out_ref[:, pl.ds(at, lanes)] = block


def collect_columns(blocks, given, core, z, planes):
    tokens, lanes = given.shape[1:]
    if lanes % 128:
        keep = [lax.dynamic_index_in_dim(block, core, 0, keepdims=False) for block in blocks]
        pairs = [[jnp.where(core == c, keep[u], given[u]) for u in range(planes)] for c in range(2)]
        return jnp.concatenate([pick(pairs[c], z ^ k) for c in range(2) for k in range(planes)], axis=1)
    vmem = pl.BlockSpec(memory_space=pltpu.VMEM)
    return pl.pallas_call(
        lambda *refs: collect_kernel(planes, *refs),
        in_specs=[pl.BlockSpec(memory_space=pltpu.SMEM)] + [vmem] * (planes + 1),
        out_specs=vmem,
        out_shape=jax.ShapeDtypeStruct((tokens, 2 * planes * lanes), BF16),
        compiler_params=pltpu.CompilerParams(vmem_limit_bytes=8 << 20),
        cost_estimate=pl.CostEstimate(flops=0, bytes_accessed=0, transcendentals=0),
        name="collect_columns",
    )(jnp.stack([core, z]).astype(jnp.int32), *blocks, given)


def local(tokens, w_in, short_filter, decay_rate, residue, skip):
    n_ctx, n_ch = lax.axis_size("ctx"), lax.axis_size("ch")
    planes = n_ctx // 2
    ctx, me = lax.axis_index("ctx"), lax.axis_index("ch")
    z, core = ctx // 2, ctx % 2
    half = w_in.shape[2] // 2
    lanes = half // planes
    groups = lanes // GROUP

    block = core * planes + z
    mine = lambda a, count, axis: lax.dynamic_slice_in_dim(a, block * count, count, axis)
    decay = mine(decay_rate, groups, 0)
    filters = long_filters(decay, mine(residue, groups, 0) * jnp.sqrt(2.0 * decay))

    w_own = w_in.transpose(1, 0, 2)
    w_sib = swap_cores(w_own, n_ctx)
    got = trade_columns(tokens, me, n_ch)
    came = trade_planes(got, z, me, planes)
    w_own, w_sib, _ = lax.optimization_barrier((w_own, w_sib, got[-1]))
    w = stage(w_own, w_sib, z, core, planes)
    taps, direct = mine(short_filter, lanes, 2), mine(skip, lanes, 0)[None]
    came, filters, w, taps, direct = lax.optimization_barrier((came, filters, w, taps, direct))
    by_plane = [pick(came, z ^ k) for k in range(planes)]
    middle = planes // 2
    x = [jnp.concatenate(by_plane[:middle], axis=0), jnp.concatenate(by_plane[middle:], axis=0)]

    order = [[], []]

    def project_pieces(stream, xs, pieces, merged):
        xs = xs + [swap_cores(y, n_ctx) for y in xs]
        order[stream].extend([(side, s, h * middle) for side in range(2) for s, h in pieces])
        return project(xs, w, planes, merged)

    near = [to_column(x[0], 1, n_ch), to_column(x[1], 2, n_ch)]
    rest = [
        to_column(jnp.concatenate([x[1], near[1]], axis=0), 1, n_ch),
        to_column(jnp.concatenate([x[0], near[0]], axis=0), 2, n_ch),
    ]
    rest += [to_column(x[h], s, n_ch) for s in range(4, n_ch) for h in range(2)]
    a, b = LineSum(planes), LineSum(planes)
    blocks = project_pieces(0, x, [(0, 0), (0, 1)], True)
    a.take_and_send(blocks)
    near = tie(blocks[-1], near)
    blocks = project_pieces(0, near, [(1, 0), (2, 1)], True)
    a.take_and_send(blocks)
    rest = tie(blocks[-1], rest)
    halves = [(1, 1), (3, 1), (2, 0), (3, 0)] + [(s, h) for s in range(4, n_ch) for h in range(2)]
    b.take(project_pieces(1, rest, halves, False))
    for t in range(planes - 2):
        for stream in (a, b):
            stream.send_even(t)
            stream.send_odd(t)
    pair, query = finish([a, b], [slice(1, 3), slice(0, 1)])
    where = jnp.stack([core, me, z]).astype(jnp.int32)
    long_out = convolve(pair, order, taps, direct, filters, where, planes, n_ch)
    outs = gate(query, order, taps, long_out, where, planes, n_ch)
    came = [to_plane(block, u, planes) if u else block for u, block in enumerate(outs)]
    given = jnp.stack([lax.dynamic_index_in_dim(block, 1 - core, 0, keepdims=False) for block in came])
    return collect_columns(came, swap_cores(given, n_ctx), core, z, planes)


def solution(mesh):
    return jax.shard_map(
        local,
        mesh=mesh,
        in_specs=(
            P("ctx", "ch"),
            P("ctx", None, "ch"),
            P(None, None, "ch"),
            P("ch", None),
            P("ch", None),
            P("ch"),
        ),
        out_specs=P("ctx", "ch"),
        check_vma=False,
    )
```
